256 devices in a mesh: dp: 64 (over y, z, core), bal: 4 (over x).
Axes of the slice: x: 4, y: 4, z: 8, core: 2. Of those that a mesh axis runs over, the one named last changes fastest.
Arguments:
- queries: bfloat16 [3, 512, 128, 1664], P(None, ('dp', 'bal')), may hold values from -30 to 30
- keys: bfloat16 [3, 512, 128, 1664], P(None, ('dp', 'bal')), may hold values from -6 to 6
- values: bfloat16 [3, 512, 128, 1664], P(None, ('dp', 'bal')), may hold values from -15 to 15
- cotangent: bfloat16 [3, 512, 128, 1664], P(None, ('dp', 'bal')), may hold values from -6 to 6
- counts: int32 [3, 64, 4], P(None, 'dp'), may hold values from 0 to 2, as said below
- out_weight: bfloat16 [1664, 1664], P('dp'), may hold values from -0.15625 to 0.15625
Outputs:
- attended: bfloat16 [3, 512, 128, 1664], P(None, ('dp', 'bal'))
- weight_grad: float32 [1664, 1664], P('dp')
The draws below stay inside these ranges and needn't reach their ends.
Inputs may be any that keep to these rules, and one draw needn't show every extreme that they name: In every micro-batch the 4 counts of one group sum to exactly 4, and one of them equals 2.
All inputs are finite; a program needn't handle non-finite values.
Results may differ from the reference program's by a relative error of at most 0.0058.
Values may be sent and summed in bfloat16 or wider, within the bound.
A program may use at most 128 MiB of HBM per device.

```python
import math
from functools import partial
import jax
import jax.numpy as jnp
from jax import lax

HEADS = 13
HD = 128
D = 1664
TT = 128
MICRO = 3
BSLOT = 1
HW = 1664
OWN = 2
GROUPS = 64
GROUP = 4
SLOTS = 512
LIVE = 98304


def draw_queries(key, part):
    own_key = jax.random.fold_in(key, 11)
    drawn = jax.random.truncated_normal(own_key, -6.0, 6.0, (MICRO, SLOTS, TT, HW), jnp.float32)
    return drawn.astype(jnp.bfloat16)


def draw_keys(key, part):
    own_key = jax.random.fold_in(key, 13)
    drawn = jax.random.truncated_normal(own_key, -6.0, 6.0, (MICRO, SLOTS, TT, HW), jnp.float32)
    return drawn.astype(jnp.bfloat16)


def draw_counts(key, part):
    key = jax.random.fold_in(key, 17)
    heavy_key, spread_key = jax.random.split(key)
    heavy = jax.random.randint(heavy_key, (MICRO, GROUPS), 0, GROUP)
    remain = GROUP * BSLOT - OWN
    picks = jax.random.randint(spread_key, (MICRO, GROUPS, remain), 0, GROUP - 1)
    target = (heavy[..., None] + 1 + picks) % GROUP
    members = jnp.arange(GROUP, dtype=jnp.int32)
    spread = jnp.sum((target[..., None] == members).astype(jnp.int32), axis=2)
    return spread + OWN * (heavy[..., None] == members).astype(jnp.int32)


def shard_levels(key, extent, pieces, smallest, high):
    level = 1.0
    for axis_at, parts in pieces:
        heights = jax.random.uniform(jax.random.fold_in(jax.random.fold_in(key, 6), axis_at), (parts,), jnp.float32, smallest / len(pieces), high / len(pieces))
        level = level * jnp.repeat(jnp.exp(heights), extent[axis_at] // parts).reshape((-1,) + (1,) * (len(extent) - 1 - axis_at))
    return level


def normal_values(key, extent, width, bound, shards=(), kind=jnp.bfloat16):
    values = jax.random.normal(key, extent, jnp.float32) * width
    if len(shards) > 0:
        values = shard_levels(key, extent, shards, -0.22, 0.18) * values
    return jnp.clip(values, min=-bound, max=bound).astype(kind)


def setup_inputs(seed: int = 0) -> dict:
    seeds = jax.random.split(jax.random.key(seed), 7)
    return {
        "queries": draw_queries(jax.random.fold_in(seeds[6], 71), 0),
        "keys": draw_keys(jax.random.fold_in(seeds[6], 71), 0),
        "values": normal_values(seeds[2], (MICRO, SLOTS, TT, HW), 2.5, 15.0, ((1, 256),)),
        "cotangent": normal_values(seeds[3], (MICRO, SLOTS, TT, D), 1.0, 6.0, ((1, 256),)),
        "counts": draw_counts(jax.random.fold_in(seeds[6], 71), 0),
        "out_weight": normal_values(seeds[5], (HW, D), HW ** -0.5, 0.15625, ((0, 64),)),
    }


def one_tile(weight, carry, tile):
    queries, keys, values, cotangent, live = tile
    shaped = (TT, HEADS, HD)
    q_float = queries.astype(jnp.float32).reshape(shaped)
    k_float = keys.astype(jnp.float32).reshape(shaped)
    v_float = values.astype(jnp.float32).reshape(shaped)
    scores = jnp.einsum('qhc,khc->hqk', q_float, k_float) * HD ** (-0.5)
    scores = scores - lax.optimization_barrier(jnp.max(scores, axis=-1, keepdims=True))
    expons = jnp.exp(scores)
    normed = (expons / lax.optimization_barrier(jnp.sum(expons, axis=-1, keepdims=True))).astype(jnp.bfloat16)
    context = jnp.einsum('hqk,khc->qhc', normed.astype(jnp.float32), v_float)
    context = context.reshape(TT, HW).astype(jnp.bfloat16)
    context = jnp.where(live > 0, context, jnp.zeros_like(context))
    attended = jnp.dot(context, weight, preferred_element_type=jnp.float32).astype(jnp.bfloat16)
    grad = carry + jnp.dot(context.T, cotangent, preferred_element_type=jnp.float32)
    return (grad, attended)

def reference(queries, keys, values, cotangent, counts, out_weight):
    position = (jnp.arange(SLOTS, dtype=jnp.int32) % OWN)[None, :]
    limits = jnp.repeat(counts.reshape(MICRO, GROUPS * GROUP), OWN, axis=1)
    live = (position < limits).astype(jnp.int32).reshape(MICRO * SLOTS)
    tiles = (queries.reshape(MICRO * SLOTS, TT, HW), keys.reshape(MICRO * SLOTS, TT, HW), values.reshape(MICRO * SLOTS, TT, HW), cotangent.reshape(MICRO * SLOTS, TT, D), live)
    start = jnp.zeros((HW, D), jnp.float32)
    grad, attended = lax.scan(partial(one_tile, out_weight), start, tiles)
    return (attended.reshape(MICRO, SLOTS, TT, D), grad / math.sqrt(LIVE))
```

```python
import math

import jax
import jax.numpy as jnp
from jax import lax
from jax.experimental import pallas as pl
from jax.experimental.pallas import tpu as pltpu
from jax.sharding import PartitionSpec as P

HEADS = 13
HD = 128
TT = 128
MICRO = 3
OWN = 2
F = 1664
ROWS = MICRO * OWN * TT
NX, NY, NZ = 4, 4, 8
HALF = 208
BLK = 26
PAD = 32
WA = 768
WB = 896
SCALE = 1.0 / math.sqrt(98304.0)
MESH = pl.DeviceIdType.MESH
F32 = jnp.float32
BF = jnp.bfloat16
NSEM = 136


def kernel(q_hbm, k_hbm, v_hbm, cot_hbm, counts, w_ref, out_hbm, grad_ref,
           q, k, v, cot, ctx, ctxt, att, wa, wb, wra, wrb,
           gs, gown, gr, gs3, gown3, gr3,
           xs2, xs1, xs3, xt0, xt1, rl1, rl2, rl3, rr1, rr2, rr3,
           ys, yr, zs, zo, zr, fr,
           in_sem, out_sem, ssem, rsem):
    dp = lax.axis_index("dp")
    x = lax.axis_index("bal")
    c = lax.rem(dp, 2)
    z = lax.rem(lax.div(dp, 2), NZ)
    y = lax.div(dp, 2 * NZ)
    sib = 1 - c
    zl = lax.rem(z, 4)
    owner = lax.div(z, 4) == c

    def dev(yy, zz, cc, xx):
        return {"dp": (yy * NZ + zz) * 2 + cc, "bal": xx}

    def at_x(d):
        return lax.rem(x + d, NX)

    def at_y(d):
        return lax.rem(y + d, NY)

    def at_z(d):
        return lax.rem(z + d, NZ)

    right_x, left_x = dev(y, z, c, at_x(1)), dev(y, z, c, at_x(3))
    up_y, down_y = dev(at_y(1), z, c, x), dev(at_y(3), z, c, x)
    up_z, down_z = dev(y, at_z(1), c, x), dev(y, at_z(7), c, x)
    sibling = dev(y, z, sib, x)

    used = [0]
    unsent = []

    def copy(src, dst, to):
        i = used[0]
        used[0] += 1
        one = pltpu.make_async_remote_copy(
            src_ref=src, dst_ref=dst, send_sem=ssem.at[i], recv_sem=rsem.at[i],
            device_id=to, device_id_type=MESH)
        one.start()
        unsent.append(one)
        return one

    loads = {}
    n_in = 0
    for m in range(MICRO):
        for name, src, dst in (("q", q_hbm, q), ("k", k_hbm, k), ("v", v_hbm, v)):
            one = pltpu.make_async_copy(src.at[pl.ds(2 * m, 2)], dst.at[pl.ds(2 * m, 2)], in_sem.at[n_in])
            one.start()
            loads[name, m] = one
            n_in += 1
    load_cot = pltpu.make_async_copy(cot_hbm, cot, in_sem.at[n_in])
    load_cot.start()

    wa[c, y, z, pl.ds(16, 16), :] = jnp.zeros((16, WA), BF)
    wb[c, y, z, pl.ds(16, 16), :] = jnp.zeros((16, WB), BF)
    wa[c, y, z, pl.ds(0, BLK), :] = w_ref[:, 0:WA]
    wb[c, y, z, pl.ds(0, BLK), :] = w_ref[:, WA:F]

    barrier = pltpu.get_barrier_semaphore()
    partners = [sibling]
    partners += [dev(y, z, cc, at_x(d)) for d in (1, 2, 3) for cc in (c, sib)]
    partners += [dev(at_y(d), z, c, x) for d in (1, 2, 3)]
    partners += [dev(y, at_z(d), c, x) for d in range(1, NZ)]
    for one in partners:
        pl.semaphore_signal(barrier, inc=1, device_id=one, device_id_type=MESH)
    pl.semaphore_wait(barrier, len(partners))

    w_sib = []

    def a_line(zz):
        return wa.at[c, :, zz]

    def a_half(zz, start):
        return wa.at[c, :, zz, pl.ds(start, 16), :]

    def b_block(zz):
        return wb.at[c, y, zz]

    def b_half(zz, start):
        return wb.at[c, y, zz, pl.ds(start, 16), :]

    def to_sib(ref):
        w_sib.append(copy(ref, ref, sibling))

    state = {}

    def a_start():
        mine = wa.at[c, y, z]
        state["ay"] = [copy(mine, mine, dev(at_y(d), z, c, x)) for d in (1, 2, 3)]

    def ring_step(key, step, whole, half):
        if step < 4:
            right = whole(at_z(8 - (step - 1)))
            left = whole(at_z(step - 1))
        else:
            right = half(at_z(5), 0)
            left = half(at_z(3), 16)
        state[key] = [copy(right, right, up_z), copy(left, left, down_z)]

    def ring_wait(key):
        for one in state[key]:
            one.wait_recv()

    def a_ring(step):
        ring_wait("ay" if step == 1 else "az")
        ring_step("az", step, a_line, a_half)
        if step == 1:
            to_sib(a_line(z))
        else:
            to_sib(a_line(at_z(8 - (step - 1))))
            to_sib(a_line(at_z(step - 1)))

    def a_end():
        ring_wait("az")
        to_sib(a_line(at_z(4)))

    def b_ring(step):
        if step > 1:
            ring_wait("bz")
        ring_step("bz", step, b_block, b_half)

    def b_y1():
        ring_wait("bz")
        line = wb.at[c, y]
        state["by"] = [copy(line, line, up_y), copy(line, line, down_y)]
        to_sib(line)

    def b_y2():
        ring_wait("by")
        below, above = at_y(3), at_y(1)
        lo = wb.at[c, below, pl.ds(0, 4)]
        hi = wb.at[c, above, pl.ds(4, 4)]
        state["by"] = [copy(lo, lo, up_y), copy(hi, hi, down_y)]
        to_sib(wb.at[c, below])
        to_sib(wb.at[c, above])

    def b_end():
        ring_wait("by")
        to_sib(wb.at[c, at_y(2)])

    def attend(m):
        for name in ("q", "k", "v"):
            loads[name, m].wait()

        def tile(j, carry):
            t = 2 * m + j
            alive = j < counts[m, 0, x]
            row = pl.multiple_of(t * TT, TT)
            for h in range(HEADS):
                cols = slice(h * HD, (h + 1) * HD)
                s = lax.dot_general(q[t, :, cols], k[t, :, cols], (((1,), (1,)), ((), ())),
                                    preferred_element_type=F32) * (HD ** -0.5)
                e = jnp.exp(s - jnp.max(s, axis=-1, keepdims=True))
                p = (e / jnp.sum(e, axis=-1, keepdims=True)).astype(BF)
                o = jnp.dot(p, v[t, :, cols], preferred_element_type=F32)
                o = jnp.where(alive, o, jnp.zeros_like(o))
                ctx[pl.ds(row, TT), cols] = o.astype(BF)
                ctxt[cols, pl.ds(row, TT)] = o.T.astype(BF)
            return carry

        lax.fori_loop(0, OWN, tile, 0)

    def grad_piece(half, col, width, store):
        def body(yy, carry):
            row = pl.multiple_of(yy * (2 * HALF) + half * HALF, 16)
            r = jnp.dot(ctxt[pl.ds(row, HALF), :], cot[:, col:col + width], preferred_element_type=F32)
            store(yy, r)
            return carry

        lax.fori_loop(0, NY, body, 0)

    def grad_sib(u):
        if u < 3:
            def store(yy, r):
                for t in range(4):
                    gs[u, t, yy] = r[:, t * 128:(t + 1) * 128].astype(BF)
            grad_piece(sib, u * 512, 512, store)
            state["g", u] = copy(gs.at[u], gr.at[u], sibling)
        else:
            def store(yy, r):
                gs3[yy] = r.astype(BF)
            grad_piece(sib, 1536, 128, store)
            state["g", u] = copy(gs3, gr3, sibling)

    def grad_own(u):
        if u < 3:
            def store(yy, r):
                for t in range(4):
                    gown[u, t, yy] = r[:, t * 128:(t + 1) * 128]
            grad_piece(c, u * 512, 512, store)
        else:
            def store(yy, r):
                gown3[yy] = r
            grad_piece(c, 1536, 128, store)

    def two(body):
        lax.fori_loop(0, 2, lambda i, carry: (body(i), carry)[1], 0)

    def x1(u):
        state["g", u].wait_recv()
        o2, o1, o3 = at_x(2), at_x(1), at_x(3)

        def pair(t, yy):
            return (gown[u, t, yy] + gr[u, t, yy].astype(F32)).astype(BF)

        def body(i):
            xs2[u, i] = pair(o2, i)
            xs2[u, i + 2] = pair(o2, i + 2)
            xs1[u, i] = pair(o1, i + 2)
            xs3[u, i] = pair(o3, i)

        two(body)
        state["x", u] = [
            copy(xs2.at[u, pl.ds(0, 2)], rl1.at[u], right_x),
            copy(xs2.at[u, pl.ds(2, 2)], rr1.at[u], left_x),
            copy(xs1.at[u], rl2.at[u], right_x),
            copy(xs3.at[u], rr2.at[u], left_x),
        ]

    def x2(u):
        state["x", u][0].wait_recv()
        state["x", u][1].wait_recv()
        o1, o3 = at_x(1), at_x(3)

        def body(i):
            xt0[u, i] = (gown[u, o1, i] + gr[u, o1, i].astype(F32) + rl1[u, i].astype(F32)).astype(BF)
            xt1[u, i] = (gown[u, o3, i + 2] + gr[u, o3, i + 2].astype(F32) + rr1[u, i].astype(F32)).astype(BF)

        two(body)
        state["x", u] += [
            copy(xt0.at[u], rl3.at[u], right_x),
            copy(xt1.at[u], rr3.at[u], left_x),
        ]

    def x3(u):
        if u < 3:
            for i in (2, 3, 4, 5):
                state["x", u][i].wait_recv()

            def body(i):
                a = (gown[u, x, i] + gr[u, x, i].astype(F32)
                     + rl3[u, i].astype(F32) + rr2[u, i].astype(F32))
                b = (gown[u, x, i + 2] + gr[u, x, i + 2].astype(F32)
                     + rl2[u, i].astype(F32) + rr3[u, i].astype(F32))
                gown[u, x, i] = a
                gown[u, x, i + 2] = b
                ys[u, i] = a.astype(BF)
                ys[u, i + 2] = b.astype(BF)
        else:
            state["g", u].wait_recv()

            def body(i):
                for j in (i, i + 2):
                    a = gown3[j] + gr3[j].astype(F32)
                    gown3[j] = a
                    ys[u, j] = a.astype(BF)

        two(body)
        state["y", u] = [
            copy(ys.at[u, at_y(d)], yr.at[u, d - 1], dev(at_y(d), z, c, x)) for d in (1, 2, 3)]

    def y2(u):
        for one in state["y", u]:
            one.wait_recv()
        total = gown[u, x, y] if u < 3 else gown3[y]
        for d in range(3):
            total = total + yr[u, d].astype(F32)
        zo[u] = total
        zs[u] = total.astype(BF)
        base = used[0]
        used[0] += 7
        copies = []
        for i in range(4):
            zt = 4 * c + i
            slot = lax.rem(z - zt + NZ, NZ) - 1
            slot = jnp.maximum(slot, 0)
            one = pltpu.make_async_remote_copy(
                src_ref=zs.at[u, pl.ds(48 * i, 64)], dst_ref=zr.at[u, slot],
                send_sem=ssem.at[base + i], recv_sem=rsem.at[base + slot],
                device_id=dev(y, zt, c, x), device_id_type=MESH)

            @pl.when(zt != z)
            def _():
                one.start()

            copies.append((zt, one))
        state["z", u] = (base, copies)

    def z2(u):
        base, copies = state["z", u]
        fbase = used[0]
        used[0] += 8

        @pl.when(owner)
        def _():
            total = zo[u, pl.ds(pl.multiple_of(48 * zl, 16), 64), :]
            for d in range(7):
                pltpu.make_async_remote_copy(
                    src_ref=zs.at[u, pl.ds(0, 64)], dst_ref=zr.at[u, d],
                    send_sem=ssem.at[base], recv_sem=rsem.at[base + d],
                    device_id=up_z, device_id_type=MESH).wait_recv()
                total = total + zr[u, d].astype(F32)
            fr[u, x] = total.astype(BF)
            n = 0
            for d in range(4):
                for cc in (c, sib):
                    if d == 0 and cc is c:
                        continue
                    pltpu.make_async_remote_copy(
                        src_ref=fr.at[u, x], dst_ref=fr.at[u, x],
                        send_sem=ssem.at[fbase + n], recv_sem=rsem.at[fbase + d],
                        device_id=dev(y, z, cc, at_x(d)), device_id_type=MESH).start()
                    n += 1

        state["f", u] = fbase

    def f2(u):
        fbase = state["f", u]

        def arrived(d):
            src = fr.at[u, at_x(4 - d)]
            pltpu.make_async_remote_copy(
                src_ref=src, dst_ref=src, send_sem=ssem.at[fbase], recv_sem=rsem.at[fbase + d],
                device_id=sibling, device_id_type=MESH).wait_recv()

        @pl.when(jnp.logical_not(owner))
        def _():
            arrived(0)

        for d in (1, 2, 3):
            arrived(d)
        if u < 3:
            for t in range(4):
                col = (4 * u + t) * 128
                grad_ref[:, col:col + 128] = fr[u, t].astype(F32) * SCALE
        else:
            total = fr[u, 0].astype(F32)
            for t in (1, 2, 3):
                total = total + fr[u, t].astype(F32)
            grad_ref[:, 1536:F] = total * SCALE

    def drain():
        for one in unsent:
            one.wait_send()
        for u in range(4):
            base, copies = state["z", u]
            for zt, one in copies:
                @pl.when(zt != z)
                def _():
                    one.wait_send()
            fbase = state["f", u]

            @pl.when(owner)
            def _():
                for n in range(7):
                    pltpu.make_async_remote_copy(
                        src_ref=fr.at[u, x], dst_ref=fr.at[u, x], send_sem=ssem.at[fbase + n],
                        recv_sem=rsem.at[fbase], device_id=sibling, device_id_type=MESH).wait_send()

    def place(src, dst, width):
        r = lax.broadcasted_iota(jnp.int32, (HALF, 8 * PAD), 0)
        s = lax.broadcasted_iota(jnp.int32, (HALF, 8 * PAD), 1)
        cc, zz, j = s // (4 * PAD), (s // PAD) % 4, s % PAD
        pick = jnp.where((j < BLK) & (r == (zz * 2 + cc) * BLK + j), 1.0, 0.0).astype(BF)

        def body(g, carry):
            yy, z0 = g // 2, (g % 2) * 4
            a = src[0, yy, pl.ds(z0, 4)].reshape(4 * PAD, width)
            b = src[1, yy, pl.ds(z0, 4)].reshape(4 * PAD, width)
            r = jnp.dot(pick, jnp.concatenate([a, b], axis=0), preferred_element_type=F32)
            dst[pl.ds(pl.multiple_of(g * HALF, 16), HALF), :] = r.astype(BF)
            return carry

        lax.fori_loop(0, 8, body, 0)

    def project(w, col, width, lo, hi):
        def body(t, carry):
            rows = pl.ds(pl.multiple_of(t * 256, 256), 256)
            r = jnp.dot(ctx[rows, :], w[...], preferred_element_type=F32)
            att[rows, col:col + width] = r.astype(BF)
            return carry

        lax.fori_loop(lo, hi, body, 0)

    out_copies = []

    def store_out(i):
        rows = pl.ds(256 * i, 256)
        one = pltpu.make_async_copy(att.at[rows], out_hbm.at[rows], out_sem.at[i])
        one.start()
        out_copies.append(one)

    a_start()
    b_ring(1)
    attend(0)
    a_ring(1)
    b_ring(2)
    attend(1)
    b_ring(3)
    attend(2)
    a_ring(2)
    b_ring(4)
    load_cot.wait()
    grad_sib(0)
    grad_own(0)
    x1(0)
    grad_sib(1)
    b_y1()
    grad_own(1)
    x1(1)
    a_ring(3)
    x2(0)
    grad_sib(2)
    grad_own(2)
    x1(2)
    grad_sib(3)
    grad_own(3)
    b_y2()
    x2(1)
    x3(0)
    a_ring(4)
    x3(3)
    x2(2)
    y2(0)
    y2(3)
    x3(1)
    b_end()
    a_end()
    z2(0)
    z2(3)
    y2(1)
    for one in w_sib:
        one.wait_recv()
    place(wa, wra, WA)
    place(wb, wrb, WB)
    x3(2)
    z2(1)
    project(wra, 0, WA, 0, 3)
    y2(2)
    project(wrb, WA, WB, 0, 1)
    store_out(0)
    z2(2)
    project(wrb, WA, WB, 1, 3)
    store_out(1)
    store_out(2)
    for u in (0, 3, 1, 2):
        f2(u)
    drain()
    for one in out_copies:
        one.wait()
    assert used[0] <= NSEM, used[0]


def core(queries, keys, values, cotangent, counts, weight):
    any_spec = pl.BlockSpec(memory_space=pl.ANY)
    vmem = pl.BlockSpec(memory_space=pltpu.VMEM)
    tiles = (MICRO * OWN, TT, F)
    V = pltpu.VMEM
    scratch = [
        V(tiles, BF), V(tiles, BF), V(tiles, BF), V((ROWS, F), BF),
        V((ROWS, F), BF), V((F, ROWS), BF), V((ROWS, F), BF),
        V((2, NY, NZ, PAD, WA), BF), V((2, NY, NZ, PAD, WB), BF), V((F, WA), BF), V((F, WB), BF),
        V((3, 4, NY, HALF, 128), BF), V((3, 4, NY, HALF, 128), F32), V((3, 4, NY, HALF, 128), BF),
        V((NY, HALF, 128), BF), V((NY, HALF, 128), F32), V((NY, HALF, 128), BF),
        V((3, 4, HALF, 128), BF),
    ]
    scratch += [V((3, 2, HALF, 128), BF)] * 10
    scratch += [
        V((4, NY, HALF, 128), BF), V((4, 3, HALF, 128), BF),
        V((4, HALF, 128), BF), V((4, HALF, 128), F32), V((4, 7, 64, 128), BF), V((4, 4, 64, 128), BF),
        pltpu.SemaphoreType.DMA((10,)), pltpu.SemaphoreType.DMA((3,)),
        pltpu.SemaphoreType.DMA((NSEM,)), pltpu.SemaphoreType.DMA((NSEM,)),
    ]
    return pl.pallas_call(
        kernel,
        out_shape=[jax.ShapeDtypeStruct((ROWS, F), BF), jax.ShapeDtypeStruct((64, F), F32)],
        in_specs=[any_spec] * 4 + [pl.BlockSpec(memory_space=pltpu.SMEM), vmem],
        out_specs=[any_spec, vmem],
        scratch_shapes=scratch,
        compiler_params=pltpu.CompilerParams(
            collective_id=0, has_side_effects=True, vmem_limit_bytes=60 * 1024 * 1024),
        cost_estimate=pl.CostEstimate(flops=9_200_000_000, bytes_accessed=20_000_000, transcendentals=1_300_000),
    )(queries, keys, values, cotangent, counts, weight)


def local(queries, keys, values, cotangent, counts, out_weight):
    tiles = (MICRO * OWN, TT, F)
    attended, rows = core(
        queries.reshape(tiles), keys.reshape(tiles), values.reshape(tiles),
        cotangent.reshape(ROWS, F), counts, out_weight)
    dp = lax.axis_index("dp")
    c, z = dp % 2, (dp // 2) % NZ
    grad = lax.dynamic_slice_in_dim(rows, 4 * (z % 4) + BLK * c, BLK, 0)
    return (attended.reshape(MICRO, OWN, TT, F), grad)


def solution(mesh):
    return jax.shard_map(
        local,
        mesh=mesh,
        in_specs=(
            P(None, ("dp", "bal"), None, None),
            P(None, ("dp", "bal"), None, None),
            P(None, ("dp", "bal"), None, None),
            P(None, ("dp", "bal"), None, None),
            P(None, "dp", None),
            P("dp", None),
        ),
        out_specs=(P(None, ("dp", "bal"), None, None), P("dp", None)),
        check_vma=False,
    )
```

```python
import math

import jax
import jax.numpy as jnp
from jax import lax
from jax.experimental import pallas as pl
from jax.experimental.pallas import tpu as pltpu
from jax.sharding import PartitionSpec as P

HEADS = 13
HD = 128
TT = 128
MICRO = 3
OWN = 2
F = 1664
ROWS = MICRO * OWN * TT
NX, NY, NZ = 4, 4, 8
HALF = 208
BLK = 26
PAD = 32
WA = 768
WB = 896
SCALE = 1.0 / math.sqrt(98304.0)
EXP_SCALE = HD ** -0.5 * 1.4426950408889634
MESH = pl.DeviceIdType.MESH
F32 = jnp.float32
BF = jnp.bfloat16
NSEM = 48


def kernel(q_hbm, k_hbm, v_hbm, cot_hbm, counts, w_ref, out_hbm, grad_ref,
           q, k, v, cot, ctx, ctxt, att, wa, wb, wra, wrb,
           gs, gown, gr, gs3, gown3, gr3,
           xs2, xs1, xs3, xt, ra, rb,
           ys, yr, zs, zo, zr, fr,
           in_sem, out_sem, ssem, rsem):
    dp = lax.axis_index("dp")
    x = lax.axis_index("bal")
    c = lax.rem(dp, 2)
    z = lax.rem(lax.div(dp, 2), NZ)
    y = lax.div(dp, 2 * NZ)
    sib = 1 - c
    zl = lax.rem(z, 4)
    owner = lax.div(z, 4) == c

    def dev(yy, zz, cc, xx):
        return {"dp": (yy * NZ + zz) * 2 + cc, "bal": xx}

    def at_x(d):
        return lax.rem(x + d, NX)

    def at_y(d):
        return lax.rem(y + d, NY)

    def at_z(d):
        return lax.rem(z + d, NZ)

    right_x, left_x = dev(y, z, c, at_x(1)), dev(y, z, c, at_x(3))
    up_y, down_y = dev(at_y(1), z, c, x), dev(at_y(3), z, c, x)
    up_z, down_z = dev(y, at_z(1), c, x), dev(y, at_z(7), c, x)
    sibling = dev(y, z, sib, x)

    ids = {}

    def sem(group):
        return ids.setdefault(group, len(ids))

    def remote(group, src, dst, to):
        i = sem(group)
        return pltpu.make_async_remote_copy(
            src_ref=src, dst_ref=dst, send_sem=ssem.at[i], recv_sem=rsem.at[i],
            device_id=to, device_id_type=MESH)

    def send(group, src, dst, to):
        remote(group, src, dst, to).start()

    sizes = {}

    def arrived(group, size):
        sizes[group] = size
        remote(group, size, size, sibling).wait_recv()

    loads = {}
    n_in = 0
    for m in range(MICRO):
        for name, src, dst in (("q", q_hbm, q), ("k", k_hbm, k), ("v", v_hbm, v)):
            one = pltpu.make_async_copy(src.at[pl.ds(2 * m, 2)], dst.at[pl.ds(2 * m, 2)], in_sem.at[n_in])
            one.start()
            loads[name, m] = one
            n_in += 1
    load_cot = pltpu.make_async_copy(cot_hbm, cot, in_sem.at[n_in])
    load_cot.start()

    barrier_sem = pltpu.get_barrier_semaphore()
    partners = [sibling]
    partners += [dev(y, z, cc, at_x(d)) for d in (1, 2, 3) for cc in (c, sib)]
    partners += [dev(at_y(d), z, c, x) for d in (1, 2, 3)]
    partners += [dev(y, at_z(d), c, x) for d in range(1, NZ)]
    for one in partners:
        pl.semaphore_signal(barrier_sem, inc=1, device_id=one, device_id_type=MESH)

    wa[c, y, 4, pl.ds(16, 16), :] = jnp.zeros((16, WA), BF)
    wb[c, y, 4, pl.ds(16, 16), :] = jnp.zeros((16, WB), BF)
    wa[c, y, 4, pl.ds(0, BLK), :] = w_ref[:, 0:WA]
    wb[c, y, 4, pl.ds(0, BLK), :] = w_ref[:, WA:F]

    def barrier():
        pl.semaphore_wait(barrier_sem, len(partners))

    def line(r):
        return wa.at[c, :, r]

    def a0():
        mine = wa.at[c, y, 4]
        for d in (1, 2, 3):
            send("ay", mine, mine, dev(at_y(d), z, c, x))

    def a_ring(step):
        if step < 4:
            send(("az", step), line(5 - step), line(4 - step), up_z)
            send(("az", step), line(3 + step), line(4 + step), down_z)
        else:
            send(("az", step), wa.at[c, :, 1, pl.ds(0, 16), :], wa.at[c, :, 0, pl.ds(0, 16), :], up_z)
            send(("az", step), wa.at[c, :, 7, pl.ds(16, 16), :], wa.at[c, :, 0, pl.ds(16, 16), :], down_z)

    def a_sib(lo, n):
        ref = wa.at[c, :, pl.ds(lo, n)]
        send("as", ref, ref, sibling)

    def a1():
        arrived("ay", wa.at[c, pl.ds(0, 3), 4])
        a_ring(1)

    def a2():
        arrived(("az", 1), wa.at[c, :, pl.ds(0, 2)])
        a_ring(2)

    def a3():
        arrived(("az", 2), wa.at[c, :, pl.ds(0, 2)])
        a_ring(3)
        a_sib(2, 5)

    def a4():
        arrived(("az", 3), wa.at[c, :, pl.ds(0, 2)])
        a_ring(4)

    def a5():
        arrived(("az", 4), line(0))
        a_sib(0, 2)
        a_sib(7, 1)

    def block(r):
        return wb.at[c, y, r]

    def b_ring(step):
        if step < 4:
            send(("bz", step), block(5 - step), block(4 - step), up_z)
            send(("bz", step), block(3 + step), block(4 + step), down_z)
        else:
            send(("bz", step), wb.at[c, y, 1, pl.ds(0, 16), :], wb.at[c, y, 0, pl.ds(0, 16), :], up_z)
            send(("bz", step), wb.at[c, y, 7, pl.ds(16, 16), :], wb.at[c, y, 0, pl.ds(16, 16), :], down_z)

    def b_pass(group, yy, lo, n, to):
        ref = wb.at[c, yy, pl.ds(lo, n)]
        send(group, ref, ref, to)

    def b0():
        b_ring(1)
        for to in (up_y, down_y):
            b_pass("by0", y, 4, 1, to)

    def b1():
        arrived(("bz", 1), wb.at[c, 0, pl.ds(0, 2)])
        b_ring(2)

    def b2():
        arrived(("bz", 2), wb.at[c, 0, pl.ds(0, 2)])
        b_ring(3)
        for to in (up_y, down_y):
            b_pass("by1", y, 2, 2, to)
            b_pass("by1", y, 5, 2, to)

    def b3():
        arrived(("bz", 3), wb.at[c, 0, pl.ds(0, 2)])
        b_ring(4)

    def b4():
        arrived(("bz", 4), block(0))
        for to in (up_y, down_y):
            b_pass("by2", y, 0, 2, to)
            b_pass("by2", y, 7, 1, to)
        b_pass("bs", y, 0, 8, sibling)

    def b5():
        arrived("by0", wb.at[c, 0, pl.ds(0, 2)])
        arrived("by1", wb.at[c, 0])
        b_pass("bw1", at_y(3), 2, 2, up_y)
        b_pass("bw1", at_y(1), 4, 3, down_y)

    def b6():
        arrived("by2", wb.at[c, 0, pl.ds(0, 6)])
        b_pass("bw2", at_y(3), 0, 2, up_y)
        b_pass("bw2", at_y(1), 7, 1, down_y)
        b_pass("bs", at_y(3), 0, 8, sibling)
        b_pass("bs", at_y(1), 0, 8, sibling)

    def b7():
        arrived("bw1", wb.at[c, 0, pl.ds(0, 5)])
        arrived("bw2", wb.at[c, 0, pl.ds(0, 3)])
        b_pass("bs", at_y(2), 0, 8, sibling)

    def attend(m):
        for name in ("q", "k", "v"):
            loads[name, m].wait()

        def tile(j, carry):
            t = 2 * m + j
            alive = j < counts[m, 0, x]
            row = pl.multiple_of(t * TT, TT)
            heads = [slice(h * HD, (h + 1) * HD) for h in range(HEADS)]
            scores = [lax.dot_general(k[t, :, h], q[t, :, h], (((1,), (1,)), ((), ())),
                                      preferred_element_type=F32) for h in heads]
            turned = [v[t, :, h].T for h in heads]
            normed = []
            for s in scores:
                e = jnp.exp2((s - jnp.max(s, axis=0, keepdims=True)) * EXP_SCALE)
                normed.append((e * (1.0 / jnp.sum(e, axis=0, keepdims=True))).astype(BF))
            parts = [jnp.dot(vt, p, preferred_element_type=F32) for vt, p in zip(turned, normed)]
            for h, o in enumerate(parts):
                o = jnp.where(alive, o, jnp.zeros_like(o)).astype(BF)
                ctx[pl.ds(row, TT), heads[h]] = o.T
                lo = h * HD
                while lo < (h + 1) * HD:
                    piece, at = lo // HALF, lo % HALF
                    hi = min((h + 1) * HD, (piece + 1) * HALF)
                    ctxt[piece % 2, pl.ds((piece // 2) * HALF + at, hi - lo), pl.ds(row, TT)] = o[lo - h * HD:hi - h * HD]
                    lo = hi
            return carry

        lax.fori_loop(0, OWN, tile, 0)

    def grad_piece(half, col, width, store):
        for j in range(0, width, 256):
            wide = min(256, width - j)
            r = jnp.dot(ctxt[half], cot[:, col + j:col + j + wide], preferred_element_type=F32)
            for t in range(0, wide, 128):
                store((j + t) // 128, r[:, t:t + 128].reshape(NY, HALF, 128))

    def grad_sib(u):
        if u == 0:
            load_cot.wait()
        if u < 3:
            def store(t, r):
                gs[u, t] = r.astype(BF)
            grad_piece(sib, u * 512, 512, store)
            send(("g", u), gs.at[u], gr.at[u], sibling)
        else:
            def store(t, r):
                gs3[...] = r.astype(BF)
            grad_piece(sib, 1536, 128, store)
            send(("g", u), gs3, gr3, sibling)

    def grad_own(u):
        if u < 3:
            def store(t, r):
                gown[u, t] = r
            grad_piece(c, u * 512, 512, store)
        else:
            def store(t, r):
                gown3[...] = r
            grad_piece(c, 1536, 128, store)

    def two(body):
        lax.fori_loop(0, 2, lambda i, carry: (body(i), carry)[1], 0)

    def pair(u, t, yy):
        return gown[u, t, yy] + gr[u, t, yy].astype(F32)

    def x1(u):
        arrived(("g", u), gr.at[u])
        o2, o1, o3 = at_x(2), at_x(1), at_x(3)

        def body(i):
            xs2[u, i] = pair(u, o2, i).astype(BF)
            xs2[u, i + 2] = pair(u, o2, i + 2).astype(BF)

        two(body)
        send(("xa", u), xs2.at[u, pl.ds(0, 2)], ra.at[u, 0], right_x)
        send(("xa", u), xs2.at[u, pl.ds(2, 2)], ra.at[u, 1], left_x)

        def body(i):
            xs1[u, i] = pair(u, o1, i + 2).astype(BF)
            xs3[u, i] = pair(u, o3, i).astype(BF)

        two(body)
        send(("xb", u), xs1.at[u], rb.at[u, 0], right_x)
        send(("xb", u), xs3.at[u], rb.at[u, 1], left_x)

    def x2(u):
        arrived(("xa", u), ra.at[u])
        o1, o3 = at_x(1), at_x(3)

        def body(i):
            xt[u, 0, i] = (pair(u, o1, i) + ra[u, 0, i].astype(F32)).astype(BF)
            xt[u, 1, i] = (pair(u, o3, i + 2) + ra[u, 1, i].astype(F32)).astype(BF)

        two(body)
        send(("xb", u), xt.at[u, 0], rb.at[u, 2], right_x)
        send(("xb", u), xt.at[u, 1], rb.at[u, 3], left_x)

    def x3(u):
        if u < 3:
            arrived(("xb", u), rb.at[u])

            def body(i):
                a = pair(u, x, i) + rb[u, 2, i].astype(F32) + rb[u, 1, i].astype(F32)
                b = pair(u, x, i + 2) + rb[u, 0, i].astype(F32) + rb[u, 3, i].astype(F32)
                gown[u, x, i] = a
                gown[u, x, i + 2] = b
                ys[u, i] = a.astype(BF)
                ys[u, i + 2] = b.astype(BF)
        else:
            arrived(("g", u), gr3)

            def body(i):
                for j in (i, i + 2):
                    a = gown3[j] + gr3[j].astype(F32)
                    gown3[j] = a
                    ys[u, j] = a.astype(BF)

        two(body)
        for d in (1, 2, 3):
            send(("y", u), ys.at[u, at_y(d)], yr.at[u, d - 1], dev(at_y(d), z, c, x))

    def y2(u):
        arrived(("y", u), yr.at[u])
        total = gown[u, x, y] if u < 3 else gown3[y]
        for d in range(3):
            total = total + yr[u, d].astype(F32)
        zo[u] = total
        zs[u] = total.astype(BF)
        for i in range(4):
            zt = 4 * c + i
            slot = jnp.maximum(lax.rem(z - zt + NZ, NZ) - 1, 0)
            one = remote(("z", u), zs.at[u, pl.ds(48 * i, 64)], zr.at[u, slot], dev(y, zt, c, x))

            @pl.when(zt != z)
            def _():
                one.start()

    def z2(u):
        sem(("f", u))

        @pl.when(owner)
        def _():
            remote(("z", u), zr.at[u], zr.at[u], sibling).wait_recv()
            total = zo[u, pl.ds(pl.multiple_of(48 * zl, 16), 64), :]
            for d in range(7):
                total = total + zr[u, d].astype(F32)
            fr[u, x] = total.astype(BF)
            for d in range(4):
                for cc in (c, sib):
                    if d == 0 and cc is c:
                        continue
                    send(("f", u), fr.at[u, x], fr.at[u, x], dev(y, z, cc, at_x(d)))

    def f2(u):
        @pl.when(owner)
        def _():
            remote(("f", u), fr.at[u, pl.ds(0, 3)], fr.at[u, pl.ds(0, 3)], sibling).wait_recv()

        @pl.when(jnp.logical_not(owner))
        def _():
            remote(("f", u), fr.at[u], fr.at[u], sibling).wait_recv()

        if u < 3:
            for t in range(4):
                col = (4 * u + t) * 128
                grad_ref[:, col:col + 128] = fr[u, t].astype(F32) * SCALE
        else:
            total = fr[u, 0].astype(F32)
            for t in (1, 2, 3):
                total = total + fr[u, t].astype(F32)
            grad_ref[:, 1536:F] = total * SCALE

    def drain():
        sizes["as"], sizes["bs"] = wa.at[c], wb.at[c]
        for group, size in sizes.items():
            remote(group, size, size, sibling).wait_send()
        for u in range(4):
            @pl.when(owner)
            def _():
                three = zr.at[u, pl.ds(0, 3)]
                remote(("z", u), three, three, sibling).wait_send()
                remote(("f", u), zr.at[u], zr.at[u], sibling).wait_send()

            @pl.when(jnp.logical_not(owner))
            def _():
                four = zr.at[u, pl.ds(0, 4)]
                remote(("z", u), four, four, sibling).wait_send()

    def place(src, dst, width, lo, hi):
        r = lax.broadcasted_iota(jnp.int32, (HALF, 8 * PAD), 0)
        s = lax.broadcasted_iota(jnp.int32, (HALF, 8 * PAD), 1)
        cc, zz, j = s // (4 * PAD), (s // PAD) % 4, s % PAD
        pick = jnp.where((j < BLK) & (r == (zz * 2 + cc) * BLK + j), 1.0, 0.0).astype(BF)

        def body(g, carry):
            yy, z0 = lax.div(g, 2), lax.rem(g, 2) * 4
            blocks = [src[cc, yy, lax.rem(z0 + i + 12 - z, NZ)] for cc in (0, 1) for i in range(4)]
            r = jnp.dot(pick, jnp.concatenate(blocks, axis=0), preferred_element_type=F32)
            dst[pl.ds(pl.multiple_of(g * HALF, 16), HALF), :] = r.astype(BF)
            return carry

        lax.fori_loop(lo, hi, body, 0)

    def place_a(i):
        if i == 0:
            arrived("as", wa.at[sib])
        place(wa, wra, WA, 4 * i, 4 * i + 4)

    def place_b(i):
        if i == 0:
            arrived("bs", wb.at[sib])
        place(wb, wrb, WB, 4 * i, 4 * i + 4)

    out_copies = []

    def project(i):
        w, col, at = (wra, 0, 256 * i) if i < 3 else (wrb, WA, 256 * (i - 3))
        wide = min(256, F - col - at)
        cols = slice(col + at, col + at + wide)
        r = jnp.dot(ctx[...], w[:, at:at + wide], preferred_element_type=F32)
        att[:, cols] = r.astype(BF)
        one = pltpu.make_async_copy(att.at[:, cols], out_hbm.at[:, cols], out_sem.at[i])
        one.start()
        out_copies.append(one)

    attend(0)
    barrier()
    a0()
    b0()
    attend(1)
    attend(2)
    grad_sib(0)
    a1()
    b1()
    grad_own(0)
    grad_sib(1)
    grad_own(1)
    grad_sib(2)
    x1(0)
    grad_own(2)
    x1(1)
    grad_sib(3)
    grad_own(3)
    x1(2)
    x3(3)
    a2()
    x2(0)
    b2()
    y2(3)
    x2(1)
    a3()
    b3()
    b5()
    z2(3)
    x2(2)
    a4()
    b4()
    x3(0)
    a5()
    x3(1)
    f2(3)
    place_a(0)
    b6()
    place_a(1)
    x3(2)
    y2(0)
    project(0)
    project(1)
    y2(1)
    project(2)
    b7()
    z2(0)
    place_b(0)
    z2(1)
    y2(2)
    place_b(1)
    project(3)
    project(4)
    project(5)
    project(6)
    z2(2)
    f2(0)
    f2(1)
    f2(2)
    drain()
    for one in out_copies:
        one.wait()
    assert len(ids) <= NSEM, len(ids)


def core(queries, keys, values, cotangent, counts, weight):
    any_spec = pl.BlockSpec(memory_space=pl.ANY)
    vmem = pl.BlockSpec(memory_space=pltpu.VMEM)
    tiles = (MICRO * OWN, TT, F)
    V = pltpu.VMEM
    scratch = [
        V(tiles, BF), V(tiles, BF), V(tiles, BF), V((ROWS, F), BF),
        V((ROWS, F), BF), V((2, NY * HALF, ROWS), BF), V((ROWS, F), BF),
        V((2, NY, NZ, PAD, WA), BF), V((2, NY, NZ, PAD, WB), BF), V((F, WA), BF), V((F, WB), BF),
        V((3, 4, NY, HALF, 128), BF), V((3, 4, NY, HALF, 128), F32), V((3, 4, NY, HALF, 128), BF),
        V((NY, HALF, 128), BF), V((NY, HALF, 128), F32), V((NY, HALF, 128), BF),
    ]
    scratch += [
        V((3, 4, HALF, 128), BF), V((3, 2, HALF, 128), BF), V((3, 2, HALF, 128), BF),
        V((3, 2, 2, HALF, 128), BF), V((3, 2, 2, HALF, 128), BF), V((3, 4, 2, HALF, 128), BF),
        V((4, NY, HALF, 128), BF), V((4, 3, HALF, 128), BF),
        V((4, HALF, 128), BF), V((4, HALF, 128), F32), V((4, 7, 64, 128), BF), V((4, 4, 64, 128), BF),
        pltpu.SemaphoreType.DMA((10,)), pltpu.SemaphoreType.DMA((7,)),
        pltpu.SemaphoreType.DMA((NSEM,)), pltpu.SemaphoreType.DMA((NSEM,)),
    ]
    return pl.pallas_call(
        kernel,
        out_shape=[jax.ShapeDtypeStruct((ROWS, F), BF), jax.ShapeDtypeStruct((64, F), F32)],
        in_specs=[any_spec] * 4 + [pl.BlockSpec(memory_space=pltpu.SMEM), vmem],
        out_specs=[any_spec, vmem],
        scratch_shapes=scratch,
        compiler_params=pltpu.CompilerParams(
            collective_id=0, has_side_effects=True, vmem_limit_bytes=60 * 1024 * 1024),
        cost_estimate=pl.CostEstimate(flops=9_200_000_000, bytes_accessed=20_000_000, transcendentals=1_300_000),
    )(queries, keys, values, cotangent, counts, weight)


def local(queries, keys, values, cotangent, counts, out_weight):
    tiles = (MICRO * OWN, TT, F)
    attended, rows = core(
        queries.reshape(tiles), keys.reshape(tiles), values.reshape(tiles),
        cotangent.reshape(ROWS, F), counts, out_weight)
    dp = lax.axis_index("dp")
    c, zl = lax.rem(dp, 2), lax.rem(lax.div(dp, 2), 4)
    grad = lax.dynamic_slice_in_dim(rows, 4 * zl + BLK * c, BLK, 0)
    return (attended.reshape(MICRO, OWN, TT, F), grad)


def solution(mesh):
    return jax.shard_map(
        local,
        mesh=mesh,
        in_specs=(
            P(None, ("dp", "bal"), None, None),
            P(None, ("dp", "bal"), None, None),
            P(None, ("dp", "bal"), None, None),
            P(None, ("dp", "bal"), None, None),
            P(None, "dp", None),
            P("dp", None),
        ),
        out_specs=(P(None, ("dp", "bal"), None, None), P("dp", None)),
        check_vma=False,
    )
```

```python
import math

import jax
import jax.numpy as jnp
from jax import lax
from jax.experimental import pallas as pl
from jax.experimental.pallas import tpu as pltpu
from jax.sharding import PartitionSpec as P

HEADS = 13
HD = 128
TT = 128
MICRO = 3
OWN = 2
F = 1664
ROWS = MICRO * OWN * TT
NX, NY, NZ = 4, 4, 8
HALF = 208
BLK = 26
PAD = 32
WA = 768
WB = 896
SCALE = 1.0 / math.sqrt(98304.0)
EXP_SCALE = HD ** -0.5 * 1.4426950408889634
MESH = pl.DeviceIdType.MESH
F32 = jnp.float32
BF = jnp.bfloat16
NSEM = 52


def kernel(q_hbm, k_hbm, v_hbm, cot_hbm, counts_hbm, w_hbm, out_hbm, grad_ref,
           counts, w_ref, q, k, v, cot, ctx, ctxt, att, wa, wb, wra, wrb,
           gs, gown, gr, gs3, gown3, gr3,
           xs2, xs1, xs3, xt, ra, rb,
           ys, yr, zs, zo, zr, fr,
           in_sem, out_sem, ssem, rsem):
    dp = lax.axis_index("dp")
    x = lax.axis_index("bal")
    c = lax.rem(dp, 2)
    z = lax.rem(lax.div(dp, 2), NZ)
    y = lax.div(dp, 2 * NZ)
    sib = 1 - c
    zl = lax.rem(z, 4)
    owner = lax.div(z, 4) == c

    def dev(yy, zz, cc, xx):
        return {"dp": (yy * NZ + zz) * 2 + cc, "bal": xx}

    def at_x(d):
        return lax.rem(x + d, NX)

    def at_y(d):
        return lax.rem(y + d, NY)

    def at_z(d):
        return lax.rem(z + d, NZ)

    right_x, left_x = dev(y, z, c, at_x(1)), dev(y, z, c, at_x(3))
    up_y, down_y = dev(at_y(1), z, c, x), dev(at_y(3), z, c, x)
    up_z, down_z = dev(y, at_z(1), c, x), dev(y, at_z(7), c, x)
    sibling = dev(y, z, sib, x)

    ids = {}

    def sem(group):
        return ids.setdefault(group, len(ids))

    def remote(group, src, dst, to):
        i = sem(group)
        return pltpu.make_async_remote_copy(
            src_ref=src, dst_ref=dst, send_sem=ssem.at[i], recv_sem=rsem.at[i],
            device_id=to, device_id_type=MESH)

    def send(group, src, dst, to):
        remote(group, src, dst, to).start()

    sizes = {}

    def arrived(group, size):
        sizes[group] = size
        remote(group, size, size, sibling).wait_recv()

    load_w = pltpu.make_async_copy(w_hbm, w_ref, in_sem.at[10])
    load_counts = pltpu.make_async_copy(counts_hbm, counts, in_sem.at[11])
    load_w.start()
    load_counts.start()
    loads = {}
    n_in = 0
    for m in range(MICRO):
        for name, src, dst in (("q", q_hbm, q), ("k", k_hbm, k), ("v", v_hbm, v)):
            one = pltpu.make_async_copy(src.at[pl.ds(2 * m, 2)], dst.at[pl.ds(2 * m, 2)], in_sem.at[n_in])
            one.start()
            loads[name, m] = one
            n_in += 1
    load_cot = pltpu.make_async_copy(cot_hbm, cot, in_sem.at[n_in])
    load_cot.start()

    barrier_sem = pltpu.get_barrier_semaphore()
    partners = [sibling]
    partners += [dev(y, z, cc, at_x(d)) for d in (1, 2, 3) for cc in (c, sib)]
    partners += [dev(at_y(d), z, c, x) for d in (1, 2, 3)]
    partners += [dev(y, at_z(d), c, x) for d in range(1, NZ)]
    for one in partners:
        pl.semaphore_signal(barrier_sem, inc=1, device_id=one, device_id_type=MESH)

    load_w.wait()
    load_counts.wait()
    for p in range(3):
        wa[p, c, y, 4, pl.ds(16, 16), :] = jnp.zeros((16, 256), BF)
        wa[p, c, y, 4, pl.ds(0, BLK), :] = w_ref[:, 256 * p:256 * p + 256]
    wb[c, y, 4, pl.ds(16, 16), :] = jnp.zeros((16, WB), BF)
    wb[c, y, 4, pl.ds(0, BLK), :] = w_ref[:, WA:F]

    def barrier():
        pl.semaphore_wait(barrier_sem, len(partners))

    def a0():
        for p in range(3):
            mine = wa.at[p, c, y, 4]
            for d in (1, 2, 3):
                send(("ay", p), mine, mine, dev(at_y(d), z, c, x))

    def a_ring(p, step):
        if step < 4:
            send(("az", p, step), wa.at[p, c, :, 5 - step], wa.at[p, c, :, 4 - step], up_z)
            send(("az", p, step), wa.at[p, c, :, 3 + step], wa.at[p, c, :, 4 + step], down_z)
        else:
            lo, hi = pl.ds(0, 16), pl.ds(16, 16)
            send(("az", p, step), wa.at[p, c, :, 1, lo, :], wa.at[p, c, :, 0, lo, :], up_z)
            send(("az", p, step), wa.at[p, c, :, 7, hi, :], wa.at[p, c, :, 0, hi, :], down_z)

    def a_sib(p, lo, n):
        ref = wa.at[p, c, :, pl.ds(lo, n)]
        send(("as", p), ref, ref, sibling)

    def a1(p):
        arrived(("ay", p), wa.at[p, c, pl.ds(0, 3), 4])
        a_ring(p, 1)

    def a2(p):
        arrived(("az", p, 1), wa.at[p, c, :, pl.ds(0, 2)])
        a_ring(p, 2)

    def a3(p):
        arrived(("az", p, 2), wa.at[p, c, :, pl.ds(0, 2)])
        a_ring(p, 3)
        a_sib(p, 2, 5)

    def a4(p):
        arrived(("az", p, 3), wa.at[p, c, :, pl.ds(0, 2)])
        a_ring(p, 4)

    def a5(p):
        arrived(("az", p, 4), wa.at[p, c, :, 0])
        a_sib(p, 0, 2)
        a_sib(p, 7, 1)

    def block(r):
        return wb.at[c, y, r]

    def b_ring(step):
        if step < 4:
            send(("bz", step), block(5 - step), block(4 - step), up_z)
            send(("bz", step), block(3 + step), block(4 + step), down_z)
        else:
            send(("bz", step), wb.at[c, y, 1, pl.ds(0, 16), :], wb.at[c, y, 0, pl.ds(0, 16), :], up_z)
            send(("bz", step), wb.at[c, y, 7, pl.ds(16, 16), :], wb.at[c, y, 0, pl.ds(16, 16), :], down_z)

    def b_pass(group, yy, lo, n, to):
        ref = wb.at[c, yy, pl.ds(lo, n)]
        send(group, ref, ref, to)

    def b0():
        b_ring(1)
        for to in (up_y, down_y):
            b_pass("by0", y, 4, 1, to)

    def b1():
        arrived(("bz", 1), wb.at[c, 0, pl.ds(0, 2)])
        b_ring(2)

    def b2():
        arrived(("bz", 2), wb.at[c, 0, pl.ds(0, 2)])
        b_ring(3)
        for to in (up_y, down_y):
            b_pass("by1", y, 2, 2, to)
            b_pass("by1", y, 5, 2, to)

    def b3():
        arrived(("bz", 3), wb.at[c, 0, pl.ds(0, 2)])
        b_ring(4)

    def b4():
        arrived(("bz", 4), block(0))
        for to in (up_y, down_y):
            b_pass("by2", y, 0, 2, to)
            b_pass("by2", y, 7, 1, to)
        b_pass("bs", y, 0, 8, sibling)

    def b5():
        arrived("by0", wb.at[c, 0, pl.ds(0, 2)])
        arrived("by1", wb.at[c, 0])
        b_pass("bw1", at_y(3), 2, 2, up_y)
        b_pass("bw1", at_y(1), 4, 3, down_y)

    def b6():
        arrived("by2", wb.at[c, 0, pl.ds(0, 6)])
        b_pass("bw2", at_y(3), 0, 2, up_y)
        b_pass("bw2", at_y(1), 7, 1, down_y)
        b_pass("bs", at_y(3), 0, 8, sibling)
        b_pass("bs", at_y(1), 0, 8, sibling)

    def b7():
        arrived("bw1", wb.at[c, 0, pl.ds(0, 5)])
        arrived("bw2", wb.at[c, 0, pl.ds(0, 3)])
        b_pass("bs", at_y(2), 0, 8, sibling)

    def attend(m):
        for name in ("q", "k", "v"):
            loads[name, m].wait()

        def tile(j, carry):
            t = 2 * m + j
            alive = j < counts[m, 0, x]
            row = pl.multiple_of(t * TT, TT)
            heads = [slice(h * HD, (h + 1) * HD) for h in range(HEADS)]
            scores = [lax.dot_general(k[t, :, h], q[t, :, h], (((1,), (1,)), ((), ())),
                                      preferred_element_type=F32) for h in heads]
            turned = [v[t, :, h].T for h in heads]
            normed = []
            for s in scores:
                e = jnp.exp2((s - jnp.max(s, axis=0, keepdims=True)) * EXP_SCALE)
                normed.append((e * (1.0 / jnp.sum(e, axis=0, keepdims=True))).astype(BF))
            parts = [jnp.dot(vt, p, preferred_element_type=F32) for vt, p in zip(turned, normed)]
            for h, o in enumerate(parts):
                o = jnp.where(alive, o, jnp.zeros_like(o)).astype(BF)
                ctx[pl.ds(row, TT), heads[h]] = o.T
                lo = h * HD
                while lo < (h + 1) * HD:
                    piece, at = lo // HALF, lo % HALF
                    hi = min((h + 1) * HD, (piece + 1) * HALF)
                    ctxt[piece % 2, pl.ds((piece // 2) * HALF + at, hi - lo), pl.ds(row, TT)] = o[lo - h * HD:hi - h * HD]
                    lo = hi
            return carry

        lax.fori_loop(0, OWN, tile, 0)

    def grad_piece(half, col, width, store):
        for j in range(0, width, 256):
            wide = min(256, width - j)
            r = jnp.dot(ctxt[half], cot[:, col + j:col + j + wide], preferred_element_type=F32)
            for t in range(0, wide, 128):
                store((j + t) // 128, r[:, t:t + 128].reshape(NY, HALF, 128))

    def grad_sib(u):
        if u == 0:
            load_cot.wait()
        if u < 3:
            def store(t, r):
                gs[u, t] = r.astype(BF)
            grad_piece(sib, u * 512, 512, store)
            send(("g", u), gs.at[u], gr.at[u], sibling)
        else:
            def store(t, r):
                gs3[...] = r.astype(BF)
            grad_piece(sib, 1536, 128, store)
            send(("g", u), gs3, gr3, sibling)

    def grad_own(u):
        if u < 3:
            def store(t, r):
                gown[u, t] = r
            grad_piece(c, u * 512, 512, store)
        else:
            def store(t, r):
                gown3[...] = r
            grad_piece(c, 1536, 128, store)

    def two(body):
        lax.fori_loop(0, 2, lambda i, carry: (body(i), carry)[1], 0)

    def pair(u, t, yy):
        return gown[u, t, yy] + gr[u, t, yy].astype(F32)

    def x1a(u):
        arrived(("g", u), gr.at[u])
        o2 = at_x(2)

        def body(i):
            xs2[u, i] = pair(u, o2, i).astype(BF)
            xs2[u, i + 2] = pair(u, o2, i + 2).astype(BF)

        two(body)
        send(("xa", u), xs2.at[u, pl.ds(0, 2)], ra.at[u, 0], right_x)
        send(("xa", u), xs2.at[u, pl.ds(2, 2)], ra.at[u, 1], left_x)

    def x1b(u):
        o1, o3 = at_x(1), at_x(3)

        def body(i):
            xs1[u, i] = pair(u, o1, i + 2).astype(BF)
            xs3[u, i] = pair(u, o3, i).astype(BF)

        two(body)
        send(("xb", u), xs1.at[u], rb.at[u, 0], right_x)
        send(("xb", u), xs3.at[u], rb.at[u, 1], left_x)

    def x2(u):
        arrived(("xa", u), ra.at[u])
        o1, o3 = at_x(1), at_x(3)

        def body(i):
            xt[u, 0, i] = (pair(u, o1, i) + ra[u, 0, i].astype(F32)).astype(BF)
            xt[u, 1, i] = (pair(u, o3, i + 2) + ra[u, 1, i].astype(F32)).astype(BF)

        two(body)
        send(("xb", u), xt.at[u, 0], rb.at[u, 2], right_x)
        send(("xb", u), xt.at[u, 1], rb.at[u, 3], left_x)

    def x3(u):
        if u < 3:
            arrived(("xb", u), rb.at[u])

            def body(i):
                a = pair(u, x, i) + rb[u, 2, i].astype(F32) + rb[u, 1, i].astype(F32)
                b = pair(u, x, i + 2) + rb[u, 0, i].astype(F32) + rb[u, 3, i].astype(F32)
                gown[u, x, i] = a
                gown[u, x, i + 2] = b
                ys[u, i] = a.astype(BF)
                ys[u, i + 2] = b.astype(BF)
        else:
            arrived(("g", u), gr3)

            def body(i):
                for j in (i, i + 2):
                    a = gown3[j] + gr3[j].astype(F32)
                    gown3[j] = a
                    ys[u, j] = a.astype(BF)

        two(body)
        for d in (1, 2, 3):
            send(("y", u), ys.at[u, at_y(d)], yr.at[u, d - 1], dev(at_y(d), z, c, x))

    def y2(u):
        arrived(("y", u), yr.at[u])
        total = gown[u, x, y] if u < 3 else gown3[y]
        for d in range(3):
            total = total + yr[u, d].astype(F32)
        zo[u] = total
        zs[u] = total.astype(BF)
        for i in range(4):
            zt = 4 * c + i
            slot = jnp.maximum(lax.rem(z - zt + NZ, NZ) - 1, 0)
            one = remote(("z", u), zs.at[u, pl.ds(48 * i, 64)], zr.at[u, slot], dev(y, zt, c, x))

            @pl.when(zt != z)
            def _():
                one.start()

    def z2(u):
        sem(("f", u))

        @pl.when(owner)
        def _():
            remote(("z", u), zr.at[u], zr.at[u], sibling).wait_recv()
            total = zo[u, pl.ds(pl.multiple_of(48 * zl, 16), 64), :]
            for d in range(7):
                total = total + zr[u, d].astype(F32)
            fr[u, x] = total.astype(BF)
            for d in range(4):
                for cc in (c, sib):
                    if d == 0 and cc is c:
                        continue
                    send(("f", u), fr.at[u, x], fr.at[u, x], dev(y, z, cc, at_x(d)))

    def f2(u):
        @pl.when(owner)
        def _():
            remote(("f", u), fr.at[u, pl.ds(0, 3)], fr.at[u, pl.ds(0, 3)], sibling).wait_recv()

        @pl.when(jnp.logical_not(owner))
        def _():
            remote(("f", u), fr.at[u], fr.at[u], sibling).wait_recv()

        if u < 3:
            for t in range(4):
                col = (4 * u + t) * 128
                grad_ref[:, col:col + 128] = fr[u, t].astype(F32) * SCALE
        else:
            total = fr[u, 0].astype(F32)
            for t in (1, 2, 3):
                total = total + fr[u, t].astype(F32)
            grad_ref[:, 1536:F] = total * SCALE

    def drain():
        sizes["bs"] = wb.at[c]
        for p in range(3):
            sizes["as", p] = wa.at[p, c]
        for group, size in sizes.items():
            remote(group, size, size, sibling).wait_send()
        for u in range(4):
            @pl.when(owner)
            def _():
                three = zr.at[u, pl.ds(0, 3)]
                remote(("z", u), three, three, sibling).wait_send()
                remote(("f", u), zr.at[u], zr.at[u], sibling).wait_send()

            @pl.when(jnp.logical_not(owner))
            def _():
                four = zr.at[u, pl.ds(0, 4)]
                remote(("z", u), four, four, sibling).wait_send()

    def place(src, dst, width, lo, hi):
        r = lax.broadcasted_iota(jnp.int32, (HALF, 8 * PAD), 0)
        s = lax.broadcasted_iota(jnp.int32, (HALF, 8 * PAD), 1)
        cc, zz, j = s // (4 * PAD), (s // PAD) % 4, s % PAD
        pick = jnp.where((j < BLK) & (r == (zz * 2 + cc) * BLK + j), 1.0, 0.0).astype(BF)

        def body(g, carry):
            yy, z0 = lax.div(g, 2), lax.rem(g, 2) * 4
            blocks = [src[cc, yy, lax.rem(z0 + i + 12 - z, NZ)] for cc in (0, 1) for i in range(4)]
            r = jnp.dot(pick, jnp.concatenate(blocks, axis=0), preferred_element_type=F32)
            dst[pl.ds(pl.multiple_of(g * HALF, 16), HALF), :] = r.astype(BF)
            return carry

        lax.fori_loop(lo, hi, body, 0)

    def place_a(p):
        arrived(("as", p), wa.at[p, sib])
        place(wa.at[p], wra.at[p], 256, 0, 8)

    def place_b(i):
        if i == 0:
            arrived("bs", wb.at[sib])
        place(wb, wrb, WB, 4 * i, 4 * i + 4)

    out_copies = []

    def project(i):
        w, col, at = (wra.at[i], 256 * i, 0) if i < 3 else (wrb, WA, 256 * (i - 3))
        wide = min(256, F - col - at)
        cols = slice(col + at, col + at + wide)
        r = jnp.dot(ctx[...], w[:, at:at + wide], preferred_element_type=F32)
        att[:, cols] = r.astype(BF)
        one = pltpu.make_async_copy(att.at[:, cols], out_hbm.at[:, cols], out_sem.at[i])
        one.start()
        out_copies.append(one)

    attend(0)
    barrier()
    b0()
    a0()
    attend(1)
    attend(2)
    b1()
    grad_sib(0)
    grad_own(0)
    grad_sib(1)
    a1(0)
    a1(1)
    a1(2)
    grad_own(1)
    x1a(0)
    x1b(0)
    b2()
    grad_sib(2)
    x1a(1)
    x1b(1)
    grad_own(2)
    a2(0)
    grad_sib(3)
    grad_own(3)
    x1a(2)
    x1b(2)
    a2(1)
    x2(0)
    x3(3)
    a2(2)
    b3()
    b5()
    a3(0)
    x2(1)
    a3(1)
    y2(3)
    a3(2)
    b4()
    a4(0)
    x2(2)
    a4(1)
    z2(3)
    b6()
    a4(2)
    a5(0)
    x3(0)
    a5(1)
    place_a(0)
    a5(2)
    place_a(1)
    x3(1)
    b7()
    place_a(2)
    project(0)
    y2(0)
    x3(2)
    project(1)
    project(2)
    y2(1)
    place_b(0)
    z2(0)
    place_b(1)
    y2(2)
    project(3)
    z2(1)
    project(4)
    project(5)
    project(6)
    f2(0)
    z2(2)
    f2(1)
    f2(3)
    f2(2)
    drain()
    for one in out_copies:
        one.wait()
    assert len(ids) <= NSEM, len(ids)


def core(queries, keys, values, cotangent, counts, weight):
    hbm = pl.BlockSpec(memory_space=pltpu.HBM)
    any_spec = pl.BlockSpec(memory_space=pl.ANY)
    vmem = pl.BlockSpec(memory_space=pltpu.VMEM)
    tiles = (MICRO * OWN, TT, F)
    V = pltpu.VMEM
    scratch = [
        pltpu.SMEM((MICRO, 1, NX), jnp.int32), V((BLK, F), BF),
        V(tiles, BF), V(tiles, BF), V(tiles, BF), V((ROWS, F), BF),
        V((ROWS, F), BF), V((2, NY * HALF, ROWS), BF), V((ROWS, F), BF),
        V((3, 2, NY, NZ, PAD, 256), BF), V((2, NY, NZ, PAD, WB), BF), V((3, F, 256), BF), V((F, WB), BF),
        V((3, 4, NY, HALF, 128), BF), V((3, 4, NY, HALF, 128), F32), V((3, 4, NY, HALF, 128), BF),
        V((NY, HALF, 128), BF), V((NY, HALF, 128), F32), V((NY, HALF, 128), BF),
    ]
    scratch += [
        V((3, 4, HALF, 128), BF), V((3, 2, HALF, 128), BF), V((3, 2, HALF, 128), BF),
        V((3, 2, 2, HALF, 128), BF), V((3, 2, 2, HALF, 128), BF), V((3, 4, 2, HALF, 128), BF),
        V((4, NY, HALF, 128), BF), V((4, 3, HALF, 128), BF),
        V((4, HALF, 128), BF), V((4, HALF, 128), F32), V((4, 7, 64, 128), BF), V((4, 4, 64, 128), BF),
        pltpu.SemaphoreType.DMA((12,)), pltpu.SemaphoreType.DMA((7,)),
        pltpu.SemaphoreType.DMA((NSEM,)), pltpu.SemaphoreType.DMA((NSEM,)),
    ]
    return pl.pallas_call(
        kernel,
        out_shape=[jax.ShapeDtypeStruct((ROWS, F), BF), jax.ShapeDtypeStruct((64, F), F32)],
        in_specs=[hbm] * 6,
        out_specs=[any_spec, vmem],
        scratch_shapes=scratch,
        compiler_params=pltpu.CompilerParams(
            collective_id=0, has_side_effects=True, vmem_limit_bytes=50 * 1024 * 1024),
        cost_estimate=pl.CostEstimate(flops=9_200_000_000, bytes_accessed=20_000_000, transcendentals=1_300_000),
    )(queries, keys, values, cotangent, counts, weight)


def local(queries, keys, values, cotangent, counts, out_weight):
    tiles = (MICRO * OWN, TT, F)
    attended, rows = core(
        queries.reshape(tiles), keys.reshape(tiles), values.reshape(tiles),
        cotangent.reshape(ROWS, F), counts, out_weight)
    dp = lax.axis_index("dp")
    c, zl = lax.rem(dp, 2), lax.rem(lax.div(dp, 2), 4)
    grad = lax.dynamic_slice_in_dim(rows, 4 * zl + BLK * c, BLK, 0)
    return (attended.reshape(MICRO, OWN, TT, F), grad)


def solution(mesh):
    return jax.shard_map(
        local,
        mesh=mesh,
        in_specs=(
            P(None, ("dp", "bal"), None, None),
            P(None, ("dp", "bal"), None, None),
            P(None, ("dp", "bal"), None, None),
            P(None, ("dp", "bal"), None, None),
            P(None, "dp", None),
            P("dp", None),
        ),
        out_specs=(P(None, ("dp", "bal"), None, None), P("dp", None)),
        check_vma=False,
    )
```

```python
import math

import jax
import jax.numpy as jnp
from jax import lax
from jax.experimental import pallas as pl
from jax.experimental.pallas import tpu as pltpu
from jax.sharding import PartitionSpec as P

HEADS = 13
HD = 128
TT = 128
MICRO = 3
OWN = 2
F = 1664
ROWS = MICRO * OWN * TT
NX, NY, NZ = 4, 4, 8
HALF = 208
BLK = 26
PAD = 32
WA = 768
WB = 896
SCALE = 1.0 / math.sqrt(98304.0)
EXP_SCALE = HD ** -0.5 * 1.4426950408889634
MESH = pl.DeviceIdType.MESH
F32 = jnp.float32
BF = jnp.bfloat16
NSEM = 52


def kernel(q_hbm, k_hbm, v_hbm, cot_hbm, counts_hbm, w_hbm, out_hbm, grad_ref,
           counts, w_ref, q, k, v, cot, ctx, ctxt, att, wa, wb, wra, wrb,
           gs, gown, gr, gs3, gown3, gr3,
           xs2, xs1, xs3, xt, ra, rb,
           ys, yr, zs, zo, zr, fr,
           in_sem, out_sem, ssem, rsem):
    dp = lax.axis_index("dp")
    x = lax.axis_index("bal")
    c = lax.rem(dp, 2)
    z = lax.rem(lax.div(dp, 2), NZ)
    y = lax.div(dp, 2 * NZ)
    sib = 1 - c
    zl = lax.rem(z, 4)
    owner = lax.div(z, 4) == c

    def dev(yy, zz, cc, xx):
        return {"dp": (yy * NZ + zz) * 2 + cc, "bal": xx}

    def at_x(d):
        return lax.rem(x + d, NX)

    def at_y(d):
        return lax.rem(y + d, NY)

    def at_z(d):
        return lax.rem(z + d, NZ)

    right_x, left_x = dev(y, z, c, at_x(1)), dev(y, z, c, at_x(3))
    up_y, down_y = dev(at_y(1), z, c, x), dev(at_y(3), z, c, x)
    up_z, down_z = dev(y, at_z(1), c, x), dev(y, at_z(7), c, x)
    sibling = dev(y, z, sib, x)

    ids = {}

    def sem(group):
        return ids.setdefault(group, len(ids))

    def remote(group, src, dst, to):
        i = sem(group)
        return pltpu.make_async_remote_copy(
            src_ref=src, dst_ref=dst, send_sem=ssem.at[i], recv_sem=rsem.at[i],
            device_id=to, device_id_type=MESH)

    def send(group, src, dst, to):
        remote(group, src, dst, to).start()

    sizes = {}

    def arrived(group, size):
        sizes[group] = size
        remote(group, size, size, sibling).wait_recv()

    load_w = pltpu.make_async_copy(w_hbm, w_ref, in_sem.at[10])
    load_counts = pltpu.make_async_copy(counts_hbm, counts, in_sem.at[11])
    load_w.start()
    load_counts.start()
    loads = {}
    n_in = 0
    for m in range(MICRO):
        for name, src, dst in (("q", q_hbm, q), ("k", k_hbm, k), ("v", v_hbm, v)):
            one = pltpu.make_async_copy(src.at[pl.ds(2 * m, 2)], dst.at[pl.ds(2 * m, 2)], in_sem.at[n_in])
            one.start()
            loads[name, m] = one
            n_in += 1
    load_cot = pltpu.make_async_copy(cot_hbm, cot, in_sem.at[n_in])
    load_cot.start()

    barrier_sem = pltpu.get_barrier_semaphore()
    partners = [sibling]
    partners += [dev(y, z, cc, at_x(d)) for d in (1, 2, 3) for cc in (c, sib)]
    partners += [dev(at_y(d), z, c, x) for d in (1, 2, 3)]
    partners += [dev(y, at_z(d), c, x) for d in range(1, NZ)]
    for one in partners:
        pl.semaphore_signal(barrier_sem, inc=1, device_id=one, device_id_type=MESH)

    load_w.wait()
    load_counts.wait()
    for p in range(3):
        wa[p, c, y, 4, pl.ds(16, 16), :] = jnp.zeros((16, 256), BF)
        wa[p, c, y, 4, pl.ds(0, BLK), :] = w_ref[:, 256 * p:256 * p + 256]
    wb[c, y, 4, pl.ds(16, 16), :] = jnp.zeros((16, WB), BF)
    wb[c, y, 4, pl.ds(0, BLK), :] = w_ref[:, WA:F]

    def barrier():
        pl.semaphore_wait(barrier_sem, len(partners))

    def a0():
        for p in range(3):
            mine = wa.at[p, c, y, 4]
            for d in (1, 2, 3):
                send(("ay", p), mine, mine, dev(at_y(d), z, c, x))

    def a_ring(p, step):
        if step < 4:
            send(("az", p, step), wa.at[p, c, :, 5 - step], wa.at[p, c, :, 4 - step], up_z)
            send(("az", p, step), wa.at[p, c, :, 3 + step], wa.at[p, c, :, 4 + step], down_z)
        else:
            lo, hi = pl.ds(0, 16), pl.ds(16, 16)
            send(("az", p, step), wa.at[p, c, :, 1, lo, :], wa.at[p, c, :, 0, lo, :], up_z)
            send(("az", p, step), wa.at[p, c, :, 7, hi, :], wa.at[p, c, :, 0, hi, :], down_z)

    def a_sib(p, lo, n):
        ref = wa.at[p, c, :, pl.ds(lo, n)]
        send(("as", p), ref, ref, sibling)

    def a1(p):
        arrived(("ay", p), wa.at[p, c, pl.ds(0, 3), 4])
        a_ring(p, 1)

    def a2(p):
        arrived(("az", p, 1), wa.at[p, c, :, pl.ds(0, 2)])
        a_ring(p, 2)

    def a3(p):
        arrived(("az", p, 2), wa.at[p, c, :, pl.ds(0, 2)])
        a_ring(p, 3)
        a_sib(p, 2, 5)

    def a4(p):
        arrived(("az", p, 3), wa.at[p, c, :, pl.ds(0, 2)])
        a_ring(p, 4)

    def a5(p):
        arrived(("az", p, 4), wa.at[p, c, :, 0])
        a_sib(p, 0, 2)
        a_sib(p, 7, 1)

    def block(r):
        return wb.at[c, y, r]

    def b_ring(step):
        if step < 4:
            send(("bz", step), block(5 - step), block(4 - step), up_z)
            send(("bz", step), block(3 + step), block(4 + step), down_z)
        else:
            send(("bz", step), wb.at[c, y, 1, pl.ds(0, 16), :], wb.at[c, y, 0, pl.ds(0, 16), :], up_z)
            send(("bz", step), wb.at[c, y, 7, pl.ds(16, 16), :], wb.at[c, y, 0, pl.ds(16, 16), :], down_z)

    def b_pass(group, yy, lo, n, to):
        ref = wb.at[c, yy, pl.ds(lo, n)]
        send(group, ref, ref, to)

    def b0():
        b_ring(1)
        for to in (up_y, down_y):
            b_pass("by0", y, 4, 1, to)

    def b1():
        arrived(("bz", 1), wb.at[c, 0, pl.ds(0, 2)])
        b_ring(2)

    def b2():
        arrived(("bz", 2), wb.at[c, 0, pl.ds(0, 2)])
        b_ring(3)
        for to in (up_y, down_y):
            b_pass("by1", y, 2, 2, to)
            b_pass("by1", y, 5, 2, to)

    def b3():
        arrived(("bz", 3), wb.at[c, 0, pl.ds(0, 2)])
        b_ring(4)

    def b4():
        arrived(("bz", 4), block(0))
        for to in (up_y, down_y):
            b_pass("by2", y, 0, 2, to)
            b_pass("by2", y, 7, 1, to)
        b_pass("bs", y, 0, 8, sibling)

    def b5():
        arrived("by0", wb.at[c, 0, pl.ds(0, 2)])
        arrived("by1", wb.at[c, 0])
        b_pass("bw1", at_y(3), 2, 2, up_y)
        b_pass("bw1", at_y(1), 4, 3, down_y)

    def b6():
        arrived("by2", wb.at[c, 0, pl.ds(0, 6)])
        b_pass("bw2", at_y(3), 0, 2, up_y)
        b_pass("bw2", at_y(1), 7, 1, down_y)
        b_pass("bs", at_y(3), 0, 8, sibling)
        b_pass("bs", at_y(1), 0, 8, sibling)

    def b7():
        arrived("bw1", wb.at[c, 0, pl.ds(0, 5)])
        arrived("bw2", wb.at[c, 0, pl.ds(0, 3)])
        b_pass("bs", at_y(2), 0, 8, sibling)

    def attend(m):
        for name in ("q", "k", "v"):
            loads[name, m].wait()

        def tile(j, carry):
            t = 2 * m + j
            alive = j < counts[m, 0, x]
            row = pl.multiple_of(t * TT, TT)
            heads = [slice(h * HD, (h + 1) * HD) for h in range(HEADS)]
            scores = [lax.dot_general(k[t, :, h], q[t, :, h], (((1,), (1,)), ((), ())),
                                      preferred_element_type=F32) for h in heads]
            turned = [v[t, :, h].T for h in heads]
            normed = []
            for s in scores:
                e = jnp.exp2((s - jnp.max(s, axis=0, keepdims=True)) * EXP_SCALE)
                normed.append((e * (1.0 / jnp.sum(e, axis=0, keepdims=True))).astype(BF))
            parts = [jnp.dot(vt, p, preferred_element_type=F32) for vt, p in zip(turned, normed)]
            for h, o in enumerate(parts):
                o = jnp.where(alive, o, jnp.zeros_like(o)).astype(BF)
                ctx[pl.ds(row, TT), heads[h]] = o.T
                lo = h * HD
                while lo < (h + 1) * HD:
                    piece, at = lo // HALF, lo % HALF
                    hi = min((h + 1) * HD, (piece + 1) * HALF)
                    ctxt[piece % 2, pl.ds((piece // 2) * HALF + at, hi - lo), pl.ds(row, TT)] = o[lo - h * HD:hi - h * HD]
                    lo = hi
            return carry

        lax.fori_loop(0, OWN, tile, 0)

    def grad_piece(half, col, width, store):
        for j in range(0, width, 256):
            wide = min(256, width - j)
            r = jnp.dot(ctxt[half], cot[:, col + j:col + j + wide], preferred_element_type=F32)
            for t in range(0, wide, 128):
                store((j + t) // 128, r[:, t:t + 128].reshape(NY, HALF, 128))

    def grad_sib(u):
        if u == 0:
            load_cot.wait()
        if u < 3:
            def store(t, r):
                gs[u, t] = r.astype(BF)
            grad_piece(sib, u * 512, 512, store)
            send(("g", u), gs.at[u], gr.at[u], sibling)
        else:
            def store(t, r):
                gs3[...] = r.astype(BF)
            grad_piece(sib, 1536, 128, store)
            send(("g", u), gs3, gr3, sibling)

    def grad_own(u):
        if u < 3:
            def store(t, r):
                gown[u, t] = r
            grad_piece(c, u * 512, 512, store)
        else:
            def store(t, r):
                gown3[...] = r
            grad_piece(c, 1536, 128, store)

    def two(body):
        lax.fori_loop(0, 2, lambda i, carry: (body(i), carry)[1], 0)

    def pair(u, t, yy):
        return gown[u, t, yy] + gr[u, t, yy].astype(F32)

    def x1a(u):
        arrived(("g", u), gr.at[u])
        o2 = at_x(2)

        def body(i):
            xs2[u, i] = pair(u, o2, i).astype(BF)
            xs2[u, i + 2] = pair(u, o2, i + 2).astype(BF)

        two(body)
        send(("xa", u), xs2.at[u, pl.ds(0, 2)], ra.at[u, 0], right_x)
        send(("xa", u), xs2.at[u, pl.ds(2, 2)], ra.at[u, 1], left_x)

    def x1b(u):
        o1, o3 = at_x(1), at_x(3)

        def body(i):
            xs1[u, i] = pair(u, o1, i + 2).astype(BF)
            xs3[u, i] = pair(u, o3, i).astype(BF)

        two(body)
        send(("xb", u), xs1.at[u], rb.at[u, 0], right_x)
        send(("xb", u), xs3.at[u], rb.at[u, 1], left_x)

    def x2(u):
        arrived(("xa", u), ra.at[u])
        o1, o3 = at_x(1), at_x(3)

        def body(i):
            xt[u, 0, i] = (pair(u, o1, i) + ra[u, 0, i].astype(F32)).astype(BF)
            xt[u, 1, i] = (pair(u, o3, i + 2) + ra[u, 1, i].astype(F32)).astype(BF)

        two(body)
        send(("xb", u), xt.at[u, 0], rb.at[u, 2], right_x)
        send(("xb", u), xt.at[u, 1], rb.at[u, 3], left_x)

    def x3(u):
        if u < 3:
            arrived(("xb", u), rb.at[u])

            def body(i):
                a = pair(u, x, i) + rb[u, 2, i].astype(F32) + rb[u, 1, i].astype(F32)
                b = pair(u, x, i + 2) + rb[u, 0, i].astype(F32) + rb[u, 3, i].astype(F32)
                gown[u, x, i] = a
                gown[u, x, i + 2] = b
                ys[u, i] = a.astype(BF)
                ys[u, i + 2] = b.astype(BF)
        else:
            arrived(("g", u), gr3)

            def body(i):
                for j in (i, i + 2):
                    a = gown3[j] + gr3[j].astype(F32)
                    gown3[j] = a
                    ys[u, j] = a.astype(BF)

        two(body)
        for d in (1, 2, 3):
            send(("y", u), ys.at[u, at_y(d)], yr.at[u, d - 1], dev(at_y(d), z, c, x))

    def y2(u):
        arrived(("y", u), yr.at[u])
        total = gown[u, x, y] if u < 3 else gown3[y]
        for d in range(3):
            total = total + yr[u, d].astype(F32)
        zo[u] = total
        zs[u] = total.astype(BF)
        for i in range(4):
            zt = 4 * c + i
            slot = jnp.maximum(lax.rem(z - zt + NZ, NZ) - 1, 0)
            one = remote(("z", u), zs.at[u, pl.ds(48 * i, 64)], zr.at[u, slot], dev(y, zt, c, x))

            @pl.when(zt != z)
            def _():
                one.start()

    def z2(u):
        sem(("f", u))

        @pl.when(owner)
        def _():
            remote(("z", u), zr.at[u], zr.at[u], sibling).wait_recv()
            total = zo[u, pl.ds(pl.multiple_of(48 * zl, 16), 64), :]
            for d in range(7):
                total = total + zr[u, d].astype(F32)
            fr[u, x] = total.astype(BF)
            for d in range(4):
                for cc in (c, sib):
                    if d == 0 and cc is c:
                        continue
                    send(("f", u), fr.at[u, x], fr.at[u, x], dev(y, z, cc, at_x(d)))

    def f2(u):
        @pl.when(owner)
        def _():
            remote(("f", u), fr.at[u, pl.ds(0, 3)], fr.at[u, pl.ds(0, 3)], sibling).wait_recv()

        @pl.when(jnp.logical_not(owner))
        def _():
            remote(("f", u), fr.at[u], fr.at[u], sibling).wait_recv()

        if u < 3:
            for t in range(4):
                col = (4 * u + t) * 128
                grad_ref[:, col:col + 128] = fr[u, t].astype(F32) * SCALE
        else:
            total = fr[u, 0].astype(F32)
            for t in (1, 2, 3):
                total = total + fr[u, t].astype(F32)
            grad_ref[:, 1536:F] = total * SCALE

    def drain(units):
        for group, size in sizes.items():
            remote(group, size, size, sibling).wait_send()
        sizes.clear()
        for u in units:
            @pl.when(owner)
            def _():
                three = zr.at[u, pl.ds(0, 3)]
                remote(("z", u), three, three, sibling).wait_send()
                remote(("f", u), zr.at[u], zr.at[u], sibling).wait_send()

            @pl.when(jnp.logical_not(owner))
            def _():
                four = zr.at[u, pl.ds(0, 4)]
                remote(("z", u), four, four, sibling).wait_send()

    def place(src, dst, width, lo, hi):
        r = lax.broadcasted_iota(jnp.int32, (HALF, 8 * PAD), 0)
        s = lax.broadcasted_iota(jnp.int32, (HALF, 8 * PAD), 1)
        cc, zz, j = s // (4 * PAD), (s // PAD) % 4, s % PAD
        pick = jnp.where((j < BLK) & (r == (zz * 2 + cc) * BLK + j), 1.0, 0.0).astype(BF)

        def body(g, carry):
            yy, z0 = lax.div(g, 2), lax.rem(g, 2) * 4
            blocks = [src[cc, yy, lax.rem(z0 + i + 12 - z, NZ)] for cc in (0, 1) for i in range(4)]
            r = jnp.dot(pick, jnp.concatenate(blocks, axis=0), preferred_element_type=F32)
            dst[pl.ds(pl.multiple_of(g * HALF, 16), HALF), :] = r.astype(BF)
            return carry

        lax.fori_loop(lo, hi, body, 0)

    def place_a(p):
        arrived(("as", p), wa.at[p, sib])
        place(wa.at[p], wra.at[p], 256, 0, 8)

    def place_b(i):
        if i == 0:
            arrived("bs", wb.at[sib])
        place(wb, wrb, WB, 4 * i, 4 * i + 4)

    out_copies = []

    def project(i):
        w, col, at = (wra.at[i], 256 * i, 0) if i < 3 else (wrb, WA, 256 * (i - 3))
        wide = min(256, F - col - at)
        cols = slice(col + at, col + at + wide)
        r = jnp.dot(ctx[...], w[:, at:at + wide], preferred_element_type=F32)
        att[:, cols] = r.astype(BF)
        one = pltpu.make_async_copy(att.at[:, cols], out_hbm.at[:, cols], out_sem.at[i])
        one.start()
        out_copies.append(one)

    attend(0)
    barrier()
    b0()
    a0()
    attend(1)
    attend(2)
    b1()
    grad_sib(0)
    grad_own(0)
    grad_sib(1)
    a1(0)
    a1(1)
    a1(2)
    grad_own(1)
    x1a(0)
    x1b(0)
    b2()
    grad_sib(2)
    x1a(1)
    x1b(1)
    grad_own(2)
    a2(0)
    grad_sib(3)
    grad_own(3)
    x1a(2)
    x1b(2)
    a2(1)
    x2(0)
    x3(3)
    a2(2)
    b3()
    b5()
    a3(0)
    x2(1)
    a3(1)
    y2(3)
    a3(2)
    b4()
    a4(0)
    x2(2)
    a4(1)
    z2(3)
    b6()
    a4(2)
    a5(0)
    x3(0)
    a5(1)
    place_a(0)
    a5(2)
    place_a(1)
    x3(1)
    b7()
    place_a(2)
    project(0)
    y2(0)
    x3(2)
    project(1)
    project(2)
    y2(1)
    place_b(0)
    z2(0)
    place_b(1)
    y2(2)
    project(3)
    z2(1)
    project(4)
    project(5)
    project(6)
    f2(0)
    z2(2)
    f2(1)
    f2(3)
    sizes["bs"] = wb.at[c]
    for p in range(3):
        sizes["as", p] = wa.at[p, c]
    drain((0, 1, 3))
    for one in out_copies:
        one.wait()
    f2(2)
    drain((2,))
    assert len(ids) <= NSEM, len(ids)


def core(queries, keys, values, cotangent, counts, weight):
    hbm = pl.BlockSpec(memory_space=pltpu.HBM)
    any_spec = pl.BlockSpec(memory_space=pl.ANY)
    vmem = pl.BlockSpec(memory_space=pltpu.VMEM)
    tiles = (MICRO * OWN, TT, F)
    V = pltpu.VMEM
    scratch = [
        pltpu.SMEM((MICRO, 1, NX), jnp.int32), V((BLK, F), BF),
        V(tiles, BF), V(tiles, BF), V(tiles, BF), V((ROWS, F), BF),
        V((ROWS, F), BF), V((2, NY * HALF, ROWS), BF), V((ROWS, F), BF),
        V((3, 2, NY, NZ, PAD, 256), BF), V((2, NY, NZ, PAD, WB), BF), V((3, F, 256), BF), V((F, WB), BF),
        V((3, 4, NY, HALF, 128), BF), V((3, 4, NY, HALF, 128), F32), V((3, 4, NY, HALF, 128), BF),
        V((NY, HALF, 128), BF), V((NY, HALF, 128), F32), V((NY, HALF, 128), BF),
    ]
    scratch += [
        V((3, 4, HALF, 128), BF), V((3, 2, HALF, 128), BF), V((3, 2, HALF, 128), BF),
        V((3, 2, 2, HALF, 128), BF), V((3, 2, 2, HALF, 128), BF), V((3, 4, 2, HALF, 128), BF),
        V((4, NY, HALF, 128), BF), V((4, 3, HALF, 128), BF),
        V((4, HALF, 128), BF), V((4, HALF, 128), F32), V((4, 7, 64, 128), BF), V((4, 4, 64, 128), BF),
        pltpu.SemaphoreType.DMA((12,)), pltpu.SemaphoreType.DMA((7,)),
        pltpu.SemaphoreType.DMA((NSEM,)), pltpu.SemaphoreType.DMA((NSEM,)),
    ]
    return pl.pallas_call(
        kernel,
        out_shape=[jax.ShapeDtypeStruct((ROWS, F), BF), jax.ShapeDtypeStruct((64, F), F32)],
        in_specs=[hbm] * 6,
        out_specs=[any_spec, vmem],
        scratch_shapes=scratch,
        compiler_params=pltpu.CompilerParams(
            collective_id=0, has_side_effects=True, vmem_limit_bytes=50 * 1024 * 1024),
        cost_estimate=pl.CostEstimate(flops=9_200_000_000, bytes_accessed=20_000_000, transcendentals=1_300_000),
    )(queries, keys, values, cotangent, counts, weight)


def local(queries, keys, values, cotangent, counts, out_weight):
    tiles = (MICRO * OWN, TT, F)
    attended, rows = core(
        queries.reshape(tiles), keys.reshape(tiles), values.reshape(tiles),
        cotangent.reshape(ROWS, F), counts, out_weight)
    dp = lax.axis_index("dp")
    c, zl = lax.rem(dp, 2), lax.rem(lax.div(dp, 2), 4)
    grad = lax.dynamic_slice_in_dim(rows, 4 * zl + BLK * c, BLK, 0)
    return (attended.reshape(MICRO, OWN, TT, F), grad)


def solution(mesh):
    return jax.shard_map(
        local,
        mesh=mesh,
        in_specs=(
            P(None, ("dp", "bal"), None, None),
            P(None, ("dp", "bal"), None, None),
            P(None, ("dp", "bal"), None, None),
            P(None, ("dp", "bal"), None, None),
            P(None, "dp", None),
            P("dp", None),
        ),
        out_specs=(P(None, ("dp", "bal"), None, None), P("dp", None)),
        check_vma=False,
    )
```

```python
import math

import jax
import jax.numpy as jnp
from jax import lax
from jax.experimental import pallas as pl
from jax.experimental.pallas import tpu as pltpu
from jax.sharding import PartitionSpec as P

HEADS = 13
HD = 128
TT = 128
MICRO = 3
OWN = 2
F = 1664
ROWS = MICRO * OWN * TT
NX, NY, NZ = 4, 4, 8
HALF = 208
BLK = 26
PAD = 32
WA = 768
WB = 896
SCALE = 1.0 / math.sqrt(98304.0)
EXP_SCALE = HD ** -0.5 * 1.4426950408889634
MESH = pl.DeviceIdType.MESH
F32 = jnp.float32
BF = jnp.bfloat16
NSEM = 52


def kernel(q_hbm, k_hbm, v_hbm, cot_hbm, counts, w_ref, out_hbm, grad_ref,
           q, k, v, cot, ctx, ctxt, att, wa, wb, wra, wrb,
           gs, gown, gr, gs3, gown3, gr3,
           xs2, xs1, xs3, xt, ra, rb,
           ys, yr, zs, zo, zr, fr,
           in_sem, out_sem, ssem, rsem):
    dp = lax.axis_index("dp")
    x = lax.axis_index("bal")
    c = lax.rem(dp, 2)
    z = lax.rem(lax.div(dp, 2), NZ)
    y = lax.div(dp, 2 * NZ)
    sib = 1 - c
    zl = lax.rem(z, 4)
    owner = lax.div(z, 4) == c

    def dev(yy, zz, cc, xx):
        return {"dp": (yy * NZ + zz) * 2 + cc, "bal": xx}

    def at_x(d):
        return lax.rem(x + d, NX)

    def at_y(d):
        return lax.rem(y + d, NY)

    def at_z(d):
        return lax.rem(z + d, NZ)

    right_x, left_x = dev(y, z, c, at_x(1)), dev(y, z, c, at_x(3))
    up_y, down_y = dev(at_y(1), z, c, x), dev(at_y(3), z, c, x)
    up_z, down_z = dev(y, at_z(1), c, x), dev(y, at_z(7), c, x)
    sibling = dev(y, z, sib, x)

    ids = {}

    def sem(group):
        return ids.setdefault(group, len(ids))

    def remote(group, src, dst, to):
        i = sem(group)
        return pltpu.make_async_remote_copy(
            src_ref=src, dst_ref=dst, send_sem=ssem.at[i], recv_sem=rsem.at[i],
            device_id=to, device_id_type=MESH)

    def send(group, src, dst, to):
        remote(group, src, dst, to).start()

    sizes = {}

    def arrived(group, size):
        sizes[group] = size
        remote(group, size, size, sibling).wait_recv()

    loads = {}
    n_in = 0
    for m in range(MICRO):
        for name, src, dst in (("q", q_hbm, q), ("k", k_hbm, k), ("v", v_hbm, v)):
            one = pltpu.make_async_copy(src.at[pl.ds(2 * m, 2)], dst.at[pl.ds(2 * m, 2)], in_sem.at[n_in])
            one.start()
            loads[name, m] = one
            n_in += 1
    load_cot = pltpu.make_async_copy(cot_hbm, cot, in_sem.at[n_in])
    load_cot.start()

    barrier_sem = pltpu.get_barrier_semaphore()
    partners = [sibling]
    partners += [dev(y, z, cc, at_x(d)) for d in (1, 2, 3) for cc in (c, sib)]
    partners += [dev(at_y(d), z, c, x) for d in (1, 2, 3)]
    partners += [dev(y, at_z(d), c, x) for d in range(1, NZ)]
    for one in partners:
        pl.semaphore_signal(barrier_sem, inc=1, device_id=one, device_id_type=MESH)

    for p in range(3):
        wa[p, c, y, 4, pl.ds(16, 16), :] = jnp.zeros((16, 256), BF)
        wa[p, c, y, 4, pl.ds(0, BLK), :] = w_ref[:, 256 * p:256 * p + 256]
    wb[c, y, 4, pl.ds(16, 16), :] = jnp.zeros((16, WB), BF)
    wb[c, y, 4, pl.ds(0, BLK), :] = w_ref[:, WA:F]

    def barrier():
        pl.semaphore_wait(barrier_sem, len(partners))

    def a0():
        for p in range(3):
            mine = wa.at[p, c, y, 4]
            for d in (1, 2, 3):
                send(("ay", p), mine, mine, dev(at_y(d), z, c, x))

    def a_ring(p, step):
        if step < 4:
            send(("az", p, step), wa.at[p, c, :, 5 - step], wa.at[p, c, :, 4 - step], up_z)
            send(("az", p, step), wa.at[p, c, :, 3 + step], wa.at[p, c, :, 4 + step], down_z)
        else:
            lo, hi = pl.ds(0, 16), pl.ds(16, 16)
            send(("az", p, step), wa.at[p, c, :, 1, lo, :], wa.at[p, c, :, 0, lo, :], up_z)
            send(("az", p, step), wa.at[p, c, :, 7, hi, :], wa.at[p, c, :, 0, hi, :], down_z)

    def a_sib(p, lo, n):
        ref = wa.at[p, c, :, pl.ds(lo, n)]
        send(("as", p), ref, ref, sibling)

    def a1(p):
        arrived(("ay", p), wa.at[p, c, pl.ds(0, 3), 4])
        a_ring(p, 1)

    def a2(p):
        arrived(("az", p, 1), wa.at[p, c, :, pl.ds(0, 2)])
        a_ring(p, 2)

    def a3(p):
        arrived(("az", p, 2), wa.at[p, c, :, pl.ds(0, 2)])
        a_ring(p, 3)
        a_sib(p, 2, 5)

    def a4(p):
        arrived(("az", p, 3), wa.at[p, c, :, pl.ds(0, 2)])
        a_ring(p, 4)

    def a5(p):
        arrived(("az", p, 4), wa.at[p, c, :, 0])
        a_sib(p, 0, 2)
        a_sib(p, 7, 1)

    def block(r):
        return wb.at[c, y, r]

    def b_ring(step):
        if step < 4:
            send(("bz", step), block(5 - step), block(4 - step), up_z)
            send(("bz", step), block(3 + step), block(4 + step), down_z)
        else:
            send(("bz", step), wb.at[c, y, 1, pl.ds(0, 16), :], wb.at[c, y, 0, pl.ds(0, 16), :], up_z)
            send(("bz", step), wb.at[c, y, 7, pl.ds(16, 16), :], wb.at[c, y, 0, pl.ds(16, 16), :], down_z)

    def b_pass(group, yy, lo, n, to):
        ref = wb.at[c, yy, pl.ds(lo, n)]
        send(group, ref, ref, to)

    def b0():
        b_ring(1)
        for to in (up_y, down_y):
            b_pass("by0", y, 4, 1, to)

    def b1():
        arrived(("bz", 1), wb.at[c, 0, pl.ds(0, 2)])
        b_ring(2)

    def b2():
        arrived(("bz", 2), wb.at[c, 0, pl.ds(0, 2)])
        b_ring(3)
        for to in (up_y, down_y):
            b_pass("by1", y, 2, 2, to)
            b_pass("by1", y, 5, 2, to)

    def b3():
        arrived(("bz", 3), wb.at[c, 0, pl.ds(0, 2)])
        b_ring(4)

    def b4():
        arrived(("bz", 4), block(0))
        for to in (up_y, down_y):
            b_pass("by2", y, 0, 2, to)
            b_pass("by2", y, 7, 1, to)
        b_pass("bs", y, 0, 8, sibling)

    def b5():
        arrived("by0", wb.at[c, 0, pl.ds(0, 2)])
        arrived("by1", wb.at[c, 0])
        b_pass("bw1", at_y(3), 2, 2, up_y)
        b_pass("bw1", at_y(1), 4, 3, down_y)

    def b6():
        arrived("by2", wb.at[c, 0, pl.ds(0, 6)])
        b_pass("bw2", at_y(3), 0, 2, up_y)
        b_pass("bw2", at_y(1), 7, 1, down_y)
        b_pass("bs", at_y(3), 0, 8, sibling)
        b_pass("bs", at_y(1), 0, 8, sibling)

    def b7():
        arrived("bw1", wb.at[c, 0, pl.ds(0, 5)])
        arrived("bw2", wb.at[c, 0, pl.ds(0, 3)])
        b_pass("bs", at_y(2), 0, 8, sibling)

    def attend(m):
        for name in ("q", "k", "v"):
            loads[name, m].wait()

        def tile(j, carry):
            t = 2 * m + j
            alive = j < counts[m, 0, x]
            row = pl.multiple_of(t * TT, TT)
            heads = [slice(h * HD, (h + 1) * HD) for h in range(HEADS)]
            scores = [lax.dot_general(k[t, :, h], q[t, :, h], (((1,), (1,)), ((), ())),
                                      preferred_element_type=F32) for h in heads]
            turned = [v[t, :, h].T for h in heads]
            normed = []
            for s in scores:
                e = jnp.exp2((s - jnp.max(s, axis=0, keepdims=True)) * EXP_SCALE)
                normed.append((e * (1.0 / jnp.sum(e, axis=0, keepdims=True))).astype(BF))
            parts = [jnp.dot(vt, p, preferred_element_type=F32) for vt, p in zip(turned, normed)]
            for h, o in enumerate(parts):
                o = jnp.where(alive, o, jnp.zeros_like(o)).astype(BF)
                ctx[pl.ds(row, TT), heads[h]] = o.T
                lo = h * HD
                while lo < (h + 1) * HD:
                    piece, at = lo // HALF, lo % HALF
                    hi = min((h + 1) * HD, (piece + 1) * HALF)
                    ctxt[piece % 2, pl.ds((piece // 2) * HALF + at, hi - lo), pl.ds(row, TT)] = o[lo - h * HD:hi - h * HD]
                    lo = hi
            return carry

        lax.fori_loop(0, OWN, tile, 0)

    def grad_piece(half, col, width, store):
        for j in range(0, width, 256):
            wide = min(256, width - j)
            r = jnp.dot(ctxt[half], cot[:, col + j:col + j + wide], preferred_element_type=F32)
            for t in range(0, wide, 128):
                store((j + t) // 128, r[:, t:t + 128].reshape(NY, HALF, 128))

    def grad_sib(u):
        if u == 0:
            load_cot.wait()
        if u < 3:
            def store(t, r):
                gs[u, t] = r.astype(BF)
            grad_piece(sib, u * 512, 512, store)
            send(("g", u), gs.at[u], gr.at[u], sibling)
        else:
            def store(t, r):
                gs3[...] = r.astype(BF)
            grad_piece(sib, 1536, 128, store)
            send(("g", u), gs3, gr3, sibling)

    def grad_own(u):
        if u < 3:
            def store(t, r):
                gown[u, t] = r
            grad_piece(c, u * 512, 512, store)
        else:
            def store(t, r):
                gown3[...] = r
            grad_piece(c, 1536, 128, store)

    def two(body):
        lax.fori_loop(0, 2, lambda i, carry: (body(i), carry)[1], 0)

    def pair(u, t, yy):
        return gown[u, t, yy] + gr[u, t, yy].astype(F32)

    def x1a(u):
        arrived(("g", u), gr.at[u])
        o2 = at_x(2)

        def body(i):
            xs2[u, i] = pair(u, o2, i).astype(BF)
            xs2[u, i + 2] = pair(u, o2, i + 2).astype(BF)

        two(body)
        send(("xa", u), xs2.at[u, pl.ds(0, 2)], ra.at[u, 0], right_x)
        send(("xa", u), xs2.at[u, pl.ds(2, 2)], ra.at[u, 1], left_x)

    def x1b(u):
        o1, o3 = at_x(1), at_x(3)

        def body(i):
            xs1[u, i] = pair(u, o1, i + 2).astype(BF)
            xs3[u, i] = pair(u, o3, i).astype(BF)

        two(body)
        send(("xb", u), xs1.at[u], rb.at[u, 0], right_x)
        send(("xb", u), xs3.at[u], rb.at[u, 1], left_x)

    def x2(u):
        arrived(("xa", u), ra.at[u])
        o1, o3 = at_x(1), at_x(3)

        def body(i):
            xt[u, 0, i] = (pair(u, o1, i) + ra[u, 0, i].astype(F32)).astype(BF)
            xt[u, 1, i] = (pair(u, o3, i + 2) + ra[u, 1, i].astype(F32)).astype(BF)

        two(body)
        send(("xb", u), xt.at[u, 0], rb.at[u, 2], right_x)
        send(("xb", u), xt.at[u, 1], rb.at[u, 3], left_x)

    def x3(u):
        if u < 3:
            arrived(("xb", u), rb.at[u])

            def body(i):
                a = pair(u, x, i) + rb[u, 2, i].astype(F32) + rb[u, 1, i].astype(F32)
                b = pair(u, x, i + 2) + rb[u, 0, i].astype(F32) + rb[u, 3, i].astype(F32)
                gown[u, x, i] = a
                gown[u, x, i + 2] = b
                ys[u, i] = a.astype(BF)
                ys[u, i + 2] = b.astype(BF)
        else:
            arrived(("g", u), gr3)

            def body(i):
                for j in (i, i + 2):
                    a = gown3[j] + gr3[j].astype(F32)
                    gown3[j] = a
                    ys[u, j] = a.astype(BF)

        two(body)
        for d in (1, 2, 3):
            send(("y", u), ys.at[u, at_y(d)], yr.at[u, d - 1], dev(at_y(d), z, c, x))

    def y2(u):
        arrived(("y", u), yr.at[u])
        total = gown[u, x, y] if u < 3 else gown3[y]
        for d in range(3):
            total = total + yr[u, d].astype(F32)
        zo[u] = total
        zs[u] = total.astype(BF)
        for i in range(4):
            zt = 4 * c + i
            slot = jnp.maximum(lax.rem(z - zt + NZ, NZ) - 1, 0)
            one = remote(("z", u), zs.at[u, pl.ds(48 * i, 64)], zr.at[u, slot], dev(y, zt, c, x))

            @pl.when(zt != z)
            def _():
                one.start()

    def z2(u):
        sem(("f", u))

        @pl.when(owner)
        def _():
            remote(("z", u), zr.at[u], zr.at[u], sibling).wait_recv()
            total = zo[u, pl.ds(pl.multiple_of(48 * zl, 16), 64), :]
            for d in range(7):
                total = total + zr[u, d].astype(F32)
            fr[u, x] = total.astype(BF)
            for d in range(4):
                for cc in (c, sib):
                    if d == 0 and cc is c:
                        continue
                    send(("f", u), fr.at[u, x], fr.at[u, x], dev(y, z, cc, at_x(d)))

    def f2(u):
        @pl.when(owner)
        def _():
            remote(("f", u), fr.at[u, pl.ds(0, 3)], fr.at[u, pl.ds(0, 3)], sibling).wait_recv()

        @pl.when(jnp.logical_not(owner))
        def _():
            remote(("f", u), fr.at[u], fr.at[u], sibling).wait_recv()

        if u < 3:
            for t in range(4):
                col = (4 * u + t) * 128
                grad_ref[:, col:col + 128] = fr[u, t].astype(F32) * SCALE
        else:
            total = fr[u, 0].astype(F32)
            for t in (1, 2, 3):
                total = total + fr[u, t].astype(F32)
            grad_ref[:, 1536:F] = total * SCALE

    def drain(units):
        for group, size in sizes.items():
            remote(group, size, size, sibling).wait_send()
        sizes.clear()
        for u in units:
            @pl.when(owner)
            def _():
                three = zr.at[u, pl.ds(0, 3)]
                remote(("z", u), three, three, sibling).wait_send()
                remote(("f", u), zr.at[u], zr.at[u], sibling).wait_send()

            @pl.when(jnp.logical_not(owner))
            def _():
                four = zr.at[u, pl.ds(0, 4)]
                remote(("z", u), four, four, sibling).wait_send()

    def place(src, dst, width, lo, hi):
        r = lax.broadcasted_iota(jnp.int32, (HALF, 8 * PAD), 0)
        s = lax.broadcasted_iota(jnp.int32, (HALF, 8 * PAD), 1)
        cc, zz, j = s // (4 * PAD), (s // PAD) % 4, s % PAD
        pick = jnp.where((j < BLK) & (r == (zz * 2 + cc) * BLK + j), 1.0, 0.0).astype(BF)

        def body(g, carry):
            yy, z0 = lax.div(g, 2), lax.rem(g, 2) * 4
            blocks = [src[cc, yy, lax.rem(z0 + i + 12 - z, NZ)] for cc in (0, 1) for i in range(4)]
            r = jnp.dot(pick, jnp.concatenate(blocks, axis=0), preferred_element_type=F32)
            dst[pl.ds(pl.multiple_of(g * HALF, 16), HALF), :] = r.astype(BF)
            return carry

        lax.fori_loop(lo, hi, body, 0)

    def place_a(p):
        arrived(("as", p), wa.at[p, sib])
        place(wa.at[p], wra.at[p], 256, 0, 8)

    def place_b(i):
        if i == 0:
            arrived("bs", wb.at[sib])
        place(wb, wrb, WB, 4 * i, 4 * i + 4)

    out_copies = []

    def project(i):
        w, col, at = (wra.at[i], 256 * i, 0) if i < 3 else (wrb, WA, 256 * (i - 3))
        wide = min(256, F - col - at)
        cols = slice(col + at, col + at + wide)
        r = jnp.dot(ctx[...], w[:, at:at + wide], preferred_element_type=F32)
        att[:, cols] = r.astype(BF)
        one = pltpu.make_async_copy(att.at[:, cols], out_hbm.at[:, cols], out_sem.at[i])
        one.start()
        out_copies.append(one)

    attend(0)
    barrier()
    b0()
    a0()
    attend(1)
    attend(2)
    b1()
    grad_sib(0)
    grad_own(0)
    grad_sib(1)
    a1(0)
    a1(1)
    a1(2)
    grad_own(1)
    x1a(0)
    x1b(0)
    b2()
    grad_sib(2)
    x1a(1)
    x1b(1)
    grad_own(2)
    a2(0)
    grad_sib(3)
    grad_own(3)
    x1a(2)
    x1b(2)
    a2(1)
    x2(0)
    x3(3)
    a2(2)
    b3()
    b5()
    a3(0)
    x2(1)
    a3(1)
    y2(3)
    a3(2)
    b4()
    a4(0)
    x2(2)
    a4(1)
    z2(3)
    b6()
    a4(2)
    a5(0)
    x3(0)
    a5(1)
    place_a(0)
    a5(2)
    place_a(1)
    x3(1)
    b7()
    place_a(2)
    project(0)
    y2(0)
    x3(2)
    project(1)
    project(2)
    y2(1)
    place_b(0)
    z2(0)
    place_b(1)
    y2(2)
    project(3)
    z2(1)
    project(4)
    project(5)
    project(6)
    f2(0)
    z2(2)
    f2(1)
    f2(3)
    sizes["bs"] = wb.at[c]
    for p in range(3):
        sizes["as", p] = wa.at[p, c]
    drain((0, 1, 3))
    for one in out_copies:
        one.wait()
    f2(2)
    drain((2,))
    assert len(ids) <= NSEM, len(ids)


def core(queries, keys, values, cotangent, counts, weight):
    hbm = pl.BlockSpec(memory_space=pltpu.HBM)
    any_spec = pl.BlockSpec(memory_space=pl.ANY)
    vmem = pl.BlockSpec(memory_space=pltpu.VMEM)
    tiles = (MICRO * OWN, TT, F)
    V = pltpu.VMEM
    scratch = [
        V(tiles, BF), V(tiles, BF), V(tiles, BF), V((ROWS, F), BF),
        V((ROWS, F), BF), V((2, NY * HALF, ROWS), BF), V((ROWS, F), BF),
        V((3, 2, NY, NZ, PAD, 256), BF), V((2, NY, NZ, PAD, WB), BF), V((3, F, 256), BF), V((F, WB), BF),
        V((3, 4, NY, HALF, 128), BF), V((3, 4, NY, HALF, 128), F32), V((3, 4, NY, HALF, 128), BF),
        V((NY, HALF, 128), BF), V((NY, HALF, 128), F32), V((NY, HALF, 128), BF),
    ]
    scratch += [
        V((3, 4, HALF, 128), BF), V((3, 2, HALF, 128), BF), V((3, 2, HALF, 128), BF),
        V((3, 2, 2, HALF, 128), BF), V((3, 2, 2, HALF, 128), BF), V((3, 4, 2, HALF, 128), BF),
        V((4, NY, HALF, 128), BF), V((4, 3, HALF, 128), BF),
        V((4, HALF, 128), BF), V((4, HALF, 128), F32), V((4, 7, 64, 128), BF), V((4, 4, 64, 128), BF),
        pltpu.SemaphoreType.DMA((10,)), pltpu.SemaphoreType.DMA((7,)),
        pltpu.SemaphoreType.DMA((NSEM,)), pltpu.SemaphoreType.DMA((NSEM,)),
    ]
    return pl.pallas_call(
        kernel,
        out_shape=[jax.ShapeDtypeStruct((ROWS, F), BF), jax.ShapeDtypeStruct((64, F), F32)],
        in_specs=[hbm] * 4 + [pl.BlockSpec(memory_space=pltpu.SMEM), vmem],
        out_specs=[any_spec, vmem],
        scratch_shapes=scratch,
        compiler_params=pltpu.CompilerParams(
            collective_id=0, has_side_effects=True, vmem_limit_bytes=50 * 1024 * 1024),
        cost_estimate=pl.CostEstimate(flops=9_200_000_000, bytes_accessed=20_000_000, transcendentals=1_300_000),
    )(queries, keys, values, cotangent, counts, weight)


def local(queries, keys, values, cotangent, counts, out_weight):
    tiles = (MICRO * OWN, TT, F)
    attended, rows = core(
        queries.reshape(tiles), keys.reshape(tiles), values.reshape(tiles),
        cotangent.reshape(ROWS, F), counts, out_weight)
    dp = lax.axis_index("dp")
    c, zl = lax.rem(dp, 2), lax.rem(lax.div(dp, 2), 4)
    grad = lax.dynamic_slice_in_dim(rows, 4 * zl + BLK * c, BLK, 0)
    return (attended.reshape(MICRO, OWN, TT, F), grad)


def solution(mesh):
    return jax.shard_map(
        local,
        mesh=mesh,
        in_specs=(
            P(None, ("dp", "bal"), None, None),
            P(None, ("dp", "bal"), None, None),
            P(None, ("dp", "bal"), None, None),
            P(None, ("dp", "bal"), None, None),
            P(None, "dp", None),
            P("dp", None),
        ),
        out_specs=(P(None, ("dp", "bal"), None, None), P("dp", None)),
        check_vma=False,
    )
```
